128 devices in a mesh: shard: 2 (over x_hi), ctx: 32 (over y, z, core), tp: 2 (over x_lo).
Axes of the slice: x: 4 (x_hi: 2, x_lo: 2; x = x_hi * 2 + x_lo), y: 4, z: 4, core: 2. Of those that a mesh axis runs over, the one named last changes fastest.
Arguments:
- tokens: bfloat16 [2, 4096, 2048], P('shard', 'ctx'), may hold values from -6 to 6
- segments: int32 [2, 4096], P('shard', 'ctx'), may hold values from 0 to 2, as said below
- decay_rate: float32 [8], P('tp'), may hold values from 2.4414063e-05 to 0.046875
- first_gain: float32 [2048], replicated, may hold values from 0.25 to 1.75
- first_bias: float32 [2048], replicated, may hold values from -3 to 3
- query_weight: bfloat16 [2048, 2048], P('shard', 'tp'), may hold values from -0.125 to 0.125
- key_weight: bfloat16 [2048, 2048], P('shard', 'tp'), may hold values from -0.125 to 0.125
- value_weight: bfloat16 [2048, 3456], P('shard', 'tp'), may hold values from -0.125 to 0.125
- gate_weight: bfloat16 [2048, 3456], P('shard', 'tp'), may hold values from -0.125 to 0.125
- out_weight: bfloat16 [3456, 2048], P('tp', 'shard'), may hold values from -0.15625 to 0.15625
- second_gain: float32 [2048], replicated, may hold values from 0.25 to 1.75
- second_bias: float32 [2048], replicated, may hold values from -3 to 3
- mlp_gate: bfloat16 [2048, 3456], P('shard', 'tp'), may hold values from -0.125 to 0.125
- mlp_up: bfloat16 [2048, 3456], P('shard', 'tp'), may hold values from -0.125 to 0.125
- mlp_down: bfloat16 [3456, 2048], P('tp', 'shard'), may hold values from -0.15625 to 0.15625
- upstream: bfloat16 [2, 4096, 2048], P('shard', 'ctx'), may hold values from -6 to 6
Outputs:
- layer_out: bfloat16 [2, 4096, 2048], P('shard', 'ctx')
- tokens_grad: float32 [2, 4096, 2048], P('shard', 'ctx')
- first_gain_grad: float32 [2048], P(('shard', 'ctx'))
- first_bias_grad: float32 [2048], P(('shard', 'ctx'))
- query_weight_grad: float32 [2048, 2048], P(('shard', 'ctx'), 'tp')
- key_weight_grad: float32 [2048, 2048], P(('shard', 'ctx'), 'tp')
- value_weight_grad: float32 [2048, 3456], P(('shard', 'ctx'), 'tp')
- gate_weight_grad: float32 [2048, 3456], P(('shard', 'ctx'), 'tp')
- out_weight_grad: float32 [3456, 2048], P('tp', ('shard', 'ctx'))
- second_gain_grad: float32 [2048], P(('shard', 'ctx'))
- second_bias_grad: float32 [2048], P(('shard', 'ctx'))
- mlp_gate_grad: float32 [2048, 3456], P(('shard', 'ctx'), 'tp')
- mlp_up_grad: float32 [2048, 3456], P(('shard', 'ctx'), 'tp')
- mlp_down_grad: float32 [3456, 2048], P('tp', ('shard', 'ctx'))
The draws below stay inside these ranges and needn't reach their ends.
Inputs may be any that keep to these rules, and one draw needn't show every extreme that they name: `segments`: segment numbers start at 0 in every sequence and rise by one at the first token of each further document; a sequence holds at most three documents. In each aligned group of 1 sequence one, chosen by the seed, holds three documents: the first of 1 to 64 tokens, the last of 1 to 64 tokens, the middle one all the rest. In the other sequences every document but the last holds at least max(2, 204) tokens.
All inputs are finite; a program needn't handle non-finite values.
Results may differ from the reference program's by a relative error of at most 0.017.
The reference program's roundings to bfloat16 on the way count: a program that leaves them out, or rounds other values in their place, can miss the bound.
Values may be sent and summed in bfloat16 or wider, within the bound.
No kernel may reach another device: no remote copies, remote signals or barrier semaphores. Data moves between devices by JAX's collectives and lax.ppermute only.
A program may use at most 320 MiB of HBM per device.

```python
import math
from functools import partial
import jax
import jax.numpy as jnp
from jax import lax

D = 2048
H = 8
KH = 256
VH = 432
FF = 3456
VW = 3456
PIECE = 128
SEQ_DEV = 1
LEN = 4096
SEQS = 2


def draw_segments(key, part):
    key = jax.random.fold_in(key, 11)
    key_len, key_edge, key_pick = jax.random.split(key, 3)
    shortest = max(2, LEN // 20)
    count = LEN // shortest + 1
    lengths = jax.random.randint(key_len, (SEQS, count), shortest, LEN + 1)
    ends = jnp.cumsum(lengths, axis=1)
    edges = jax.random.randint(key_edge, (SEQS, 2), 1, PIECE // 2 + 1)
    filler = jnp.full((SEQS, count - 2), 2 * LEN + 1, jnp.int32)
    spanning = jnp.concatenate([edges[:, :1], LEN - edges[:, 1:], filler], axis=1).astype(jnp.int32)
    chosen = jax.random.randint(key_pick, (SEQS // SEQ_DEV,), 0, SEQ_DEV)
    picked = jnp.arange(SEQS) % SEQ_DEV == jnp.repeat(chosen, SEQ_DEV)
    bounds = jnp.where(picked[:, None], spanning, ends.astype(jnp.int32))
    place = jnp.arange(LEN)
    numbers = jnp.sum((bounds[:, :, None] <= place[None, None, :]).astype(jnp.int32), axis=1)
    return jnp.minimum(numbers, 2).astype(jnp.int32)


def raised(values, key, source, target, blocks, factor):
    owner, partner = [(jnp.arange(values.shape[position]) // (values.shape[position] // blocks)).reshape([-1 if axis == position else 1 for axis in range(values.ndim)]) for position in (source, target)]
    chosen = jax.random.permutation(key, blocks)[partner]
    strong = (owner == chosen) | (owner == (partner + blocks // 2) % blocks)
    return jnp.where(strong, factor * values, values)


def block_scale(own_key, extent, shards, low, top_value):
    loudness = 1.0
    for position, blocks in shards:
        heights = jax.random.uniform(jax.random.fold_in(jax.random.fold_in(own_key, 6), position), (blocks,), jnp.float32, low / len(shards), top_value / len(shards))
        loudness = loudness * jnp.repeat(jnp.exp(heights), extent[position] // blocks).reshape((-1,) + (1,) * (len(extent) - 1 - position))
    return loudness


def centred(key, dims, spread, limit, cuts=(), kind=jnp.bfloat16):
    loudness = block_scale(key, dims, cuts, -0.22, 0.18) if cuts else 1.0
    entries = jax.random.normal(key, dims, jnp.float32) * spread * loudness
    return jnp.minimum(jnp.maximum(entries, -limit), limit).astype(kind)


def bell_draw_with(stream_key, extent, spread, limit, cuts, heavy, dtype=jnp.bfloat16):
    values = spread * jax.random.normal(stream_key, extent, jnp.float32)
    if cuts:
        values = values * block_scale(stream_key, extent, cuts, -0.22, 0.18)
    return jnp.clip(raised(values, jax.random.fold_in(stream_key, 3), *heavy), -limit, limit).astype(dtype)


def setup_inputs(seed: int = 0) -> dict:
    seeds = jax.random.split(jax.random.key(seed), 17)
    tokens = centred(seeds[0], (SEQS, LEN, D), 1.0, 6.0, ((0, 2), (1, 32)))
    segments = draw_segments(jax.random.fold_in(seeds[16], 71), 0)
    decay_rate = jnp.clip(jnp.exp(math.log(0.046875) - 7.5600805 * jax.random.uniform(seeds[2], (H,), jnp.float32) ** block_scale(seeds[2], (H,), ((0, 2),), -0.2, 0.2)), 2.441406286379788e-05, 0.046875)
    first_gain = jnp.clip(1.0 + 0.15 * jax.random.normal(seeds[3], (D,), jnp.float32), 0.25, 1.75)
    first_bias = centred(seeds[4], (D,), 0.5, 3.0, (), jnp.float32)
    query_weight = centred(seeds[5], (D, H * KH), D ** -0.5, 0.125, ((0, 2), (1, 2)))
    key_weight = centred(seeds[6], (D, H * KH), D ** -0.5, 0.125, ((0, 2), (1, 2)))
    value_weight = centred(seeds[7], (D, VW), D ** -0.5, 0.125, ((0, 2), (1, 2)))
    gate_weight = centred(seeds[8], (D, VW), D ** -0.5, 0.125, ((0, 2), (1, 2)))
    out_weight = centred(seeds[9], (VW, D), (VW // 2) ** -0.5, 0.15625, ((0, 2), (1, 2)))
    second_gain = jnp.clip(1.0 + 0.15 * jax.random.normal(seeds[10], (D,), jnp.float32), 0.25, 1.75)
    second_bias = centred(seeds[11], (D,), 0.5, 3.0, (), jnp.float32)
    mlp_gate = centred(seeds[12], (D, FF), D ** -0.5, 0.125, ((0, 2), (1, 2)))
    mlp_up = centred(seeds[13], (D, FF), D ** -0.5, 0.125, ((0, 2), (1, 2)))
    mlp_down = centred(seeds[14], (FF, D), (FF // 2) ** -0.5, 0.15625, ((0, 2), (1, 2)))
    upstream = bell_draw_with(seeds[15], (SEQS, LEN, D), 1.0, 6.0, ((0, 2), (1, 32)), (1, 2, 32, 2.75))
    return dict(tokens=tokens, segments=segments, decay_rate=decay_rate, first_gain=first_gain, first_bias=first_bias, query_weight=query_weight, key_weight=key_weight, value_weight=value_weight, gate_weight=gate_weight, out_weight=out_weight, second_gain=second_gain, second_bias=second_bias, mlp_gate=mlp_gate, mlp_up=mlp_up, mlp_down=mlp_down, upstream=upstream)


EPS = 1e-05
HIGHEST_ACCURACY = lax.Precision.HIGHEST

@jax.custom_vjp
def low(v):
    return lax.optimization_barrier(v.astype(jnp.bfloat16)).astype(jnp.float32)

@jax.custom_vjp
def low_back(v):
    return v

def low_keep(v):
    return (low(v), None)

def low_pass(kept, grad):
    return (grad,)

def back_keep(v):
    return (v, None)

def back_low(kept, grad):
    return (low(grad),)
low.defvjp(low_keep, low_pass)
low_back.defvjp(back_keep, back_low)

def product(left, right):
    return jnp.dot(left, right, precision=HIGHEST_ACCURACY)

def norm_rows(values):
    center = values - lax.optimization_barrier(jnp.mean(values, -1, keepdims=True))
    return center * lax.rsqrt(lax.optimization_barrier(jnp.mean(center * center, -1, keepdims=True)) + EPS)

def retention_piece(rate, carry, piece_data):
    running_state, last = carry
    query_vector, key_row_block, value_vector, seg = piece_data
    count = seg.shape[0]
    place = jnp.arange(count)
    offset = place[:, None] - place[None, :]
    valid = (offset >= 0) & (seg[:, None] == seg[None, :])
    decay = jnp.where(valid[None], jnp.exp(-rate[:, None, None] * jnp.maximum(offset, 0).astype(jnp.float32)[None]), 0.0)
    scores = low_back(jnp.einsum('ihk,jhk->hij', query_vector, key_row_block, precision=HIGHEST_ACCURACY))
    masked = low(scores * decay)
    inner = jnp.einsum('hij,jhv->ihv', masked, value_vector, precision=HIGHEST_ACCURACY)
    reach_extent = jnp.exp(-rate[None, :] * (place + 1).astype(jnp.float32)[:, None]) * (seg == last).astype(jnp.float32)[:, None]
    outer_across = reach_extent[:, :, None] * jnp.einsum('jls,lsp->jlp', query_vector, running_state, precision=HIGHEST_ACCURACY)
    retained = low_back(inner + outer_across)
    tail_portion = jnp.exp(-rate[None, :] * (count - 1 - place).astype(jnp.float32)[:, None]) * (seg == seg[-1]).astype(jnp.float32)[:, None]
    local_within = jnp.einsum('mna,mnw->naw', key_row_block * tail_portion[:, :, None], value_vector, precision=HIGHEST_ACCURACY)
    keep = jnp.where((seg[0] == last) & (seg[0] == seg[-1]), jnp.exp(-rate * count), 0.0)
    return ((local_within + keep[:, None, None] * running_state, seg[-1]), retained)

def forward(inputs, first_gain, first_bias, query_weight, key_weight, value_weight, gate_weight, out_weight, second_gain, second_bias, mlp_gate, mlp_up, mlp_down, seg, rate):
    length = inputs.shape[0]
    pieces = length // PIECE
    heads = rate.shape[0]
    lowered_first = low(norm_rows(inputs) * first_gain + first_bias)
    queries = low(low_back(product(lowered_first, query_weight))).reshape(pieces, PIECE, heads, KH)
    keys_all = low(low_back(product(lowered_first, key_weight))).reshape(pieces, PIECE, heads, KH)
    values = low(low_back(product(lowered_first, value_weight))).reshape(pieces, PIECE, heads, VH)
    gate_pre = low_back(product(lowered_first, gate_weight))
    step_fn = jax.checkpoint(partial(retention_piece, rate))
    start = (jnp.zeros((heads, KH, VH), jnp.float32), jnp.array(-1, jnp.int32))
    _, retained = lax.scan(step_fn, start, (queries, keys_all, values, seg.reshape(pieces, PIECE)))
    grouped = norm_rows(retained).reshape(length, heads * VH)
    mixed = low(jax.nn.silu(gate_pre) * grouped)
    middle = inputs + low_back(product(mixed, out_weight))
    lowered_second = low(norm_rows(middle) * second_gain + second_bias)
    up_gate = low_back(product(lowered_second, mlp_gate))
    up_vals = low_back(product(lowered_second, mlp_up))
    hidden = low(jax.nn.silu(up_gate) * up_vals)
    return middle + low_back(product(hidden, mlp_down))

def add_pair(left, right):
    return left + right

def reference(tokens, segments, decay_rate, first_gain, first_bias, query_weight, key_weight, value_weight, gate_weight, out_weight, second_gain, second_bias, mlp_gate, mlp_up, mlp_down, upstream):
    params = tuple((p.astype(jnp.float32) for p in (first_gain, first_bias, query_weight, key_weight, value_weight, gate_weight, out_weight, second_gain, second_bias, mlp_gate, mlp_up, mlp_down)))

    def per_sequence(total, item):
        inputs, seg, cotangent = item

        def forward_of(values, *weights):
            return forward(values, *weights, seg, decay_rate)
        result, pull = jax.vjp(forward_of, inputs.astype(jnp.float32), *params)
        grads = pull(cotangent.astype(jnp.float32))
        total = jax.tree.map(add_pair, total, tuple(grads[1:]))
        return (total, (result.astype(jnp.bfloat16), grads[0]))
    zeros = tuple((jnp.zeros_like(p) for p in params))
    total, outputs = lax.scan(per_sequence, zeros, (tokens, segments, upstream))
    return (outputs[0], outputs[1], total[0], total[1], total[2], total[3], total[4], total[5], total[6], total[7], total[8], total[9], total[10], total[11])
```

```python
import functools

import jax
import jax.numpy as jnp
from jax import lax
from jax.experimental import pallas as pl
from jax.experimental.pallas import tpu as pltpu
from jax.sharding import PartitionSpec as P

KH = 256
VH = 432
EPS = 1e-05
BF = jnp.bfloat16
F32 = jnp.float32
F16 = jnp.float16
NC = 32
BLOCK = 32
HALF = 1024
VW = 1728
VPAD = 1792
HEADS = 4
PIECE = 128
QKV = 2 * HALF + VW
GATHERED = 3
PACKED = GATHERED * VPAD
WIDE = 2048

SWAP = [(0, 1), (1, 0)]
CORE = [(index, index ^ 1) for index in range(NC)]
SHARD_TP = [(0, 3), (1, 2), (2, 1), (3, 0)]
SHARD_CORE = [(index, (index ^ 1) ^ NC) for index in range(2 * NC)]
PLANE = [[2 * chip + core for chip in range(16)] for core in range(2)]
ANY = pl.BlockSpec(memory_space=pl.ANY)
SMEM = pl.BlockSpec(memory_space=pltpu.SMEM)


def product(left, right):
    return jnp.dot(left, right, preferred_element_type=F32)


def product_left(left, right):
    return lax.dot_general(left, right, (((0,), (0,)), ((), ())), preferred_element_type=F32)


def product_right(left, right):
    return lax.dot_general(left, right, (((1,), (1,)), ((), ())), preferred_element_type=F32)


def from_shard(part):
    return lax.ppermute(part, "shard", SWAP)


def half_from_shard(part):
    return lax.ppermute(part.astype(F16), "shard", SWAP).astype(F32)


def from_tp(part):
    return lax.ppermute(part, "tp", SWAP)


def core_swap(part):
    return lax.ppermute(part, "ctx", CORE)


def shape(*dims, kind=BF):
    return jax.ShapeDtypeStruct(dims, kind)


def whole(array):
    return pl.BlockSpec(array.shape, lambda i, rank=len(array.shape): (0,) * rank)


def run(kernel, outs, scalars, blocks, far=(), scratch=(), flops=0):
    single = not isinstance(outs, tuple)
    outs = (outs,) if single else outs
    got = pl.pallas_call(
        kernel,
        out_shape=outs,
        grid=(1,),
        in_specs=[SMEM] * len(scalars) + [whole(a) for a in blocks] + [ANY] * len(far),
        out_specs=tuple(whole(a) for a in outs),
        scratch_shapes=list(scratch),
        compiler_params=pltpu.CompilerParams(vmem_limit_bytes=56 * 1024 * 1024),
        cost_estimate=pl.CostEstimate(flops=flops, bytes_accessed=0, transcendentals=0),
    )(*scalars, *blocks, *far)
    return got[0] if single else got


def hold(arrays, *others):
    count = len(arrays)
    return pl.pallas_call(
        lambda *refs: None,
        out_shape=tuple(shape(*a.shape, kind=a.dtype) for a in arrays),
        in_specs=[ANY] * (count + len(others)),
        out_specs=(ANY,) * count,
        input_output_aliases={k: k for k in range(count)},
        cost_estimate=pl.CostEstimate(flops=0, bytes_accessed=0, transcendentals=0),
    )(*arrays, *others)


def after(array, *others):
    return hold((array,), *others)[0]


def fetch(sources, holders, semaphores):
    copies = [pltpu.make_async_copy(src, dst, semaphores.at[k]) for k, (src, dst) in enumerate(zip(sources, holders))]
    for copy in copies:
        copy.start()
    return copies


def part_of(others, k):
    return others.at[:, k * VPAD : (k + 1) * VPAD]


def own_first(shard, array):
    a, b = array[:, :HALF], array[:, HALF:]
    return jnp.where(shard == 0, a, b), jnp.where(shard == 0, b, a)


def normed_of(own, oth):
    mean = (jnp.sum(own, 1, keepdims=True) + jnp.sum(oth, 1, keepdims=True)) / WIDE
    own, oth = own - mean, oth - mean
    var = (jnp.sum(own * own, 1, keepdims=True) + jnp.sum(oth * oth, 1, keepdims=True)) / WIDE
    inverse = lax.rsqrt(var + EPS)
    return own * inverse, oth * inverse, inverse


def norm_back(grads, gains, normed, inverse):
    grads = [grad * gain for grad, gain in zip(grads, gains)]
    mean = sum(jnp.sum(g, 1, keepdims=True) for g in grads) / WIDE
    slant = sum(jnp.sum(g * n, 1, keepdims=True) for g, n in zip(grads, normed)) / WIDE
    return [inverse * (g - mean - n * slant) for g, n in zip(grads, normed)]


def first_kernel(place, shard, tokens, gain, bias, *refs):
    weights, (normed, inverse, low_own, low_oth, packed, columns, semaphores) = refs[:GATHERED], refs[GATHERED:]
    begin = pl.multiple_of(place[0] // 4 * 128, 128)
    copies = fetch([w.at[:, pl.ds(begin, 128)] for w in weights], [columns.at[k] for k in range(GATHERED)], semaphores)
    own, oth = own_first(shard[0], tokens[...].astype(F32))
    own, oth, scale = normed_of(own, oth)
    gains, biases = own_first(shard[0], gain[...]), own_first(shard[0], bias[...])
    normed[:, :HALF] = own
    normed[:, HALF:] = oth
    inverse[...] = jnp.broadcast_to(scale, inverse.shape)
    low_own[...] = (own * gains[0] + biases[0]).astype(BF)
    low_oth[...] = (oth * gains[1] + biases[1]).astype(BF)
    packed[...] = jnp.zeros_like(packed)
    column = lax.broadcasted_iota(jnp.int32, (BLOCK, 128), 1)
    wanted = lax.broadcasted_iota(jnp.int32, (BLOCK, 128), 0) + (place[0] % 4) * BLOCK
    chosen = (column == wanted).astype(F32).astype(BF)
    for k in range(GATHERED):
        copies[k].wait()
        packed[:, k * VPAD : k * VPAD + VW] = product_right(chosen, columns[k]).astype(BF)


def turn_kernel(shard, array, own, oth):
    own[...], oth[...] = own_first(shard[0], array[...])


def help_kernel(low, key_weight, value_weight, key, value):
    key[...] = product(low[...], key_weight[...])
    value[...] = product_right(low[...], value_weight[...])


def help_more_kernel(low, query_weight, gate_weight, query, gate):
    query[...] = product(low[...], query_weight[...])
    gate[...] = product_right(low[...], gate_weight[...])


def base_kernel(low, query_weight, key_weight, value_weight, gate_weight, _, query, key, value, gate):
    query[...] = product(low[...], query_weight[...])
    key[...] = product(low[...], key_weight[...])
    value[...] = product_right(low[...], value_weight[...])
    gate[...] = product_right(low[...], gate_weight[...])


def hidden_kernel(own, theirs, weight, base, helped):
    both = jnp.concatenate([own[...], theirs[...]], 0)
    total = product_right(both, weight[...])
    base[...] = total[:PIECE]
    helped[...] = total[PIECE:]


def window(head):
    begin = head * VH // 128 * 128
    end = -(-(head + 1) * VH // 128) * 128
    return begin, end


def inside(head, rows):
    begin, end = window(head)
    column = lax.broadcasted_iota(jnp.int32, (rows, end - begin), 1) + begin
    return (column >= head * VH) & (column < (head + 1) * VH)


def head_part(ref, head, rows):
    begin, end = window(head)
    return jnp.where(inside(head, rows), ref[:, begin:end].astype(F32), 0.0)


def decay_of(rate, seg_column, seg_row):
    down = lax.broadcasted_iota(jnp.int32, (PIECE, PIECE), 0) - lax.broadcasted_iota(jnp.int32, (PIECE, PIECE), 1)
    near = jnp.exp(-rate * jnp.maximum(down, 0).astype(F32))
    return jnp.where((down >= 0) & (seg_column == seg_row), near, 0.0)


def tail_of(rate, seg_column, seg_row):
    left = (PIECE - 1 - lax.broadcasted_iota(jnp.int32, (PIECE, 1), 0)).astype(F32)
    return jnp.where(seg_column == seg_row[:, PIECE - 1 :], jnp.exp(-rate * left), 0.0)


def reach_of(rate, seg_column, before):
    passed = (lax.broadcasted_iota(jnp.int32, (PIECE, 1), 0) + 1).astype(F32)
    return jnp.where(seg_column == before, jnp.exp(-rate * passed), 0.0)


def with_marks(total, seg_row):
    column = lax.broadcasted_iota(jnp.int32, total.shape, 1)
    marked = jnp.where(column == VW, seg_row[:, :1], jnp.where(column == VW + 1, seg_row[:, PIECE - 1 :], 0.0))
    return jnp.where(column < VW, total, marked).astype(BF)


def mark(states, offset):
    column = lax.broadcasted_iota(jnp.int32, (states.shape[0], 128), 1)
    return jnp.sum(jnp.where(column == VW - (VPAD - 128) + offset, states[:, VPAD - 128 :], 0.0), 1, keepdims=True)


def local_kernel(rates, seg_column, seg_row, base_key, base_value, helped_key, helped_value, _, keys, values, local, total):
    keys[...] = (base_key[...] + helped_key[...].astype(F32)).astype(BF)
    values[:, :VW] = (base_value[...] + helped_value[...].astype(F32)).astype(BF)
    values[:, VW:] = jnp.zeros((PIECE, VPAD - VW), BF)
    total[...] = jnp.zeros_like(total)
    for head in range(HEADS):
        begin, end = window(head)
        own = slice(head * KH, (head + 1) * KH)
        value = head_part(values, head, PIECE).astype(BF)
        key_tail = (keys[:, own].astype(F32) * tail_of(rates[head], seg_column[...], seg_row[...])).astype(BF)
        total[:, begin:end] += product_left(key_tail, value)
    local[...] = with_marks(total[...], seg_row[...])


def inner_kernel(rates, seg_column, seg_row, base_query, helped_query, keys, values, queries, inner, masked):
    queries[...] = (base_query[...] + helped_query[...].astype(F32)).astype(BF)
    inner[...] = jnp.zeros_like(inner)
    for head in range(HEADS):
        begin, end = window(head)
        own = slice(head * KH, (head + 1) * KH)
        scores = product_right(queries[:, own], keys[:, own])
        kept = (scores * decay_of(rates[head], seg_column[...], seg_row[...])).astype(BF)
        masked[head] = kept
        inner[:, begin:end] += product(kept, head_part(values, head, PIECE).astype(BF))


def scan_kernel(reverse, rates, states, *refs):
    out = refs[-1]
    column = lax.broadcasted_iota(jnp.int32, (8, VPAD), 1)
    rate = jnp.full((8, VPAD), rates[HEADS - 1], F32)
    for head in range(HEADS - 1):
        rate = jnp.where((column >= head * VH) & (column < (head + 1) * VH), rates[head], rate)
    factor = jnp.exp(-rate * PIECE)
    edges = [states[p, :, VPAD - 128 :].astype(F32) for p in range(NC)]

    def mark_of(p, offset):
        lane = lax.broadcasted_iota(jnp.int32, (8, 128), 1)
        return jnp.sum(jnp.where(lane == VW - (VPAD - 128) + offset, edges[p], 0.0), 1, keepdims=True)

    firsts = [mark_of(p, 0) for p in range(NC)]
    lasts = [mark_of(p, 1) for p in range(NC)]
    befores = [jnp.full((8, 1), -1.0, F32)] + lasts[:-1]
    carry = jnp.zeros((8, VPAD), F32)
    for k in range(NC):
        p = NC - 1 - k if reverse else k
        out[p] = jnp.where(column < VW, carry, befores[p]).astype(BF)
        keep = jnp.where((firsts[p] == lasts[p]) & (firsts[p] == befores[p]), factor, 0.0)
        carry = states[p].astype(F32) + keep * carry


def mix_kernel(
    rates, seg_column, queries, inner, incoming, base_gate, helped_gate, out_weight, others, _,
    gate, grouped, inverse, mixed, part, total, held, near, semaphores,
):
    copies = fetch([out_weight, part_of(others, 2)], [near, held], semaphores)
    gate[...] = base_gate[...] + helped_gate[...].astype(F32)
    before = mark(incoming[:16].astype(F32), 0)[:1]
    total[...] = inner[...]
    for head in range(HEADS):
        begin, end = window(head)
        own = slice(head * KH, (head + 1) * KH)
        across = product(queries[:, own], incoming[:, begin:end])
        total[:, begin:end] += jnp.where(
            inside(head, PIECE), reach_of(rates[head], seg_column[...], before) * across, 0.0
        )
    lane = lax.broadcasted_iota(jnp.int32, (PIECE, 128), 1)
    scales = jnp.zeros((PIECE, 128), F32)
    grouped[...] = jnp.zeros_like(grouped)
    for head in range(HEADS):
        begin, end = window(head)
        here = inside(head, PIECE)
        retained = jnp.where(here, total[:, begin:end], 0.0)
        center = jnp.where(here, retained - jnp.sum(retained, 1, keepdims=True) / VH, 0.0)
        scale = lax.rsqrt(jnp.sum(center * center, 1, keepdims=True) / VH + EPS)
        grouped[:, begin:end] += center * scale
        scales = jnp.where(lane == head, scale, scales)
    inverse[...] = scales
    mixed[:, :VW] = (jax.nn.silu(gate[...]) * grouped[:, :VW]).astype(BF)
    mixed[:, VW:] = jnp.zeros((PIECE, VPAD - VW), BF)
    copies[0].wait()
    part[:, :HALF] = product(mixed[:, :VW], near[...]).astype(BF)
    copies[1].wait()
    part[:, HALF:] = product_right(mixed[...], held[...]).astype(BF)


def mlp_kernel(
    shard, tokens, mine, theirs, gain, bias, base_hidden, helped_hidden, mixed, gate_weight, up_weight, others, _up, _low,
    middle, normed, inverse, low_own, low_oth, grads, part,
    near_gate, near_up, far_gate, far_up, semaphores,
):
    copies = fetch(
        [gate_weight, part_of(others, 0), up_weight, part_of(others, 1)],
        [near_gate, far_gate, near_up, far_up],
        semaphores,
    )
    own, oth = own_first(shard[0], tokens[...].astype(F32))
    own = own + (mine[:, :HALF].astype(F32) + theirs[:, :HALF].astype(F32))
    oth = oth + (mine[:, HALF:].astype(F32) + theirs[:, HALF:].astype(F32))
    middle[:, :HALF] = own
    middle[:, HALF:] = oth
    own, oth, scale = normed_of(own, oth)
    gains, biases = own_first(shard[0], gain[...]), own_first(shard[0], bias[...])
    normed[:, :HALF] = own
    normed[:, HALF:] = oth
    inverse[...] = jnp.broadcast_to(scale, inverse.shape)
    low_own[...] = (own * gains[0] + biases[0]).astype(BF)
    low_oth[...] = (oth * gains[1] + biases[1]).astype(BF)
    copies[0].wait()
    up_gate = product_right(low_own[...], near_gate[...])
    copies[1].wait()
    up_gate += product(low_oth[...], far_gate[:, :VW])
    copies[2].wait()
    up_vals = product_right(low_own[...], near_up[...])
    copies[3].wait()
    up_vals += product(low_oth[...], far_up[:, :VW])
    grad_hidden = base_hidden[...] + helped_hidden[...].astype(F32)
    sigma = jax.nn.sigmoid(up_gate)
    silu = up_gate * sigma
    none = jnp.zeros((PIECE, VPAD - VW), BF)
    for k, array in enumerate(
        (silu * up_vals, grad_hidden * up_vals * (sigma * (1.0 + up_gate * (1.0 - sigma))), grad_hidden * silu)
    ):
        grads[:, k * VPAD : k * VPAD + VW] = array.astype(BF)
        grads[:, k * VPAD + VW : (k + 1) * VPAD] = none
    grads[:, 3 * VPAD :] = mixed[...]
    total = product(grads[:, VPAD : VPAD + VW], near_gate[...])
    total += product(grads[:, 2 * VPAD : 2 * VPAD + VW], near_up[...])
    part[:, :HALF] = total.astype(BF)
    total = product_right(grads[:, VPAD : 2 * VPAD], far_gate[...])
    total += product_right(grads[:, 2 * VPAD : 3 * VPAD], far_up[...])
    part[:, HALF:] = total.astype(BF)


def down_kernel(own, theirs, weight, part):
    both = jnp.concatenate([own[:, :VW], theirs[:, :VW]], 0)
    part[...] = product(both, weight[...]).astype(BF)


def down_sum_kernel(mine, theirs, own, gone):
    own[...] = mine[:PIECE].astype(F32) + theirs[:PIECE].astype(F32)
    gone[...] = (mine[PIECE:].astype(F32) + theirs[PIECE:].astype(F32)).astype(BF)


def result_kernel(shard, middle, own, oth, out):
    total = [middle[:, :HALF] + own[...], middle[:, HALF:] + oth[...].astype(F32)]
    out[:, :HALF] = jnp.where(shard[0] == 0, total[0], total[1]).astype(BF)
    out[:, HALF:] = jnp.where(shard[0] == 0, total[1], total[0]).astype(BF)


def unmix_kernel(
    shard, rates, mine, theirs, normed, inverse, gain, up_own, up_oth, seg_column, seg_row, queries, incoming, gate,
    grouped, scales, out_weight, others,
    grad_middle, branch_own, branch_oth, vectors, grad_gate, grad_retained, term,
    held, total, near, far, semaphores,
):
    copies = fetch([out_weight, part_of(others, 2)], [near, far], semaphores)
    grads = [mine[:, cut].astype(F32) + theirs[:, cut].astype(F32) for cut in (slice(0, HALF), slice(HALF, WIDE))]
    norms = [normed[:, :HALF], normed[:, HALF:]]
    vectors[...] = jnp.zeros_like(vectors)
    for k in range(2):
        cut = slice(k * HALF, (k + 1) * HALF)
        vectors[0:1, cut] = jnp.sum(grads[k] * norms[k], 0, keepdims=True)
        vectors[1:2, cut] = jnp.sum(grads[k], 0, keepdims=True)
    back = norm_back(grads, own_first(shard[0], gain[...]), norms, inverse[:, :1])
    own, oth = up_own[...].astype(F32) + back[0], up_oth[...].astype(F32) + back[1]
    grad_middle[:, :HALF] = own
    grad_middle[:, HALF:] = oth
    branch_own[...] = own.astype(BF)
    branch_oth[...] = oth.astype(BF)
    before = mark(incoming[:16].astype(F32), 0)[:1]
    sigma = jax.nn.sigmoid(gate[...])
    copies[0].wait()
    grad_mixed = product_right(branch_own[...], near[...])
    copies[1].wait()
    grad_mixed += product(branch_oth[...], far[:, :VW])
    slope = sigma * (1.0 + gate[...] * (1.0 - sigma))
    none = jnp.zeros((PIECE, VPAD - VW), F32)
    grad_gate[:, :VW] = (grad_mixed * grouped[:, :VW] * slope).astype(BF)
    grad_gate[:, VW:] = none.astype(BF)
    held[:, :VW] = grad_mixed * (gate[...] * sigma)
    held[:, VW:] = none
    lane = lax.broadcasted_iota(jnp.int32, (PIECE, 128), 1)
    total[...] = jnp.zeros_like(total)
    for head in range(HEADS):
        begin, end = window(head)
        here = inside(head, PIECE)
        grad = head_part(held, head, PIECE)
        group = head_part(grouped, head, PIECE)
        scale = jnp.sum(jnp.where(lane == head, scales[...], 0.0), 1, keepdims=True)
        back = grad - jnp.sum(grad, 1, keepdims=True) / VH - group * (jnp.sum(grad * group, 1, keepdims=True) / VH)
        total[:PIECE, begin:end] += jnp.where(here, scale * back, 0.0)
    grad_retained[...] = total[:PIECE].astype(BF)
    total[...] = jnp.zeros_like(total)
    for head in range(HEADS):
        begin, end = window(head)
        own = slice(head * KH, (head + 1) * KH)
        reached = reach_of(rates[head], seg_column[...], before) * head_part(grad_retained, head, PIECE)
        total[:, begin:end] += product_left(queries[:, own], reached.astype(BF))
    term[...] = with_marks(total[...], seg_row[...])


def back_kernel(
    rates, seg_column, seg_row, queries, keys, values, masked, incoming, grad_retained, grad_gate, gb, low2,
    gate_query, parcel, base_key, base_value,
):
    before = mark(incoming[:16].astype(F32), 0)[:1]
    gate_query[:, :VPAD] = grad_gate[...]
    base_value[...] = jnp.zeros_like(base_value)
    for head in range(HEADS):
        rate = rates[head]
        begin, end = window(head)
        own = slice(head * KH, (head + 1) * KH)
        value = head_part(values, head, PIECE).astype(BF)
        grad = head_part(grad_retained, head, PIECE).astype(BF)
        decay = decay_of(rate, seg_column[...], seg_row[...])
        reach = reach_of(rate, seg_column[...], before)
        grad_scores = (product_right(grad, value) * decay).astype(BF)
        grad_query = product(grad_scores, keys[:, own])
        grad_query += reach * product_right(grad, incoming[:, begin:end])
        gate_query[:, VPAD + head * KH : VPAD + (head + 1) * KH] = grad_query.astype(BF)
        base_key[:, own] = product_left(grad_scores, queries[:, own])
        base_value[:, begin:end] += product_left(masked[head], grad)
    parcel[:, :HALF] = gb[...]
    parcel[:, HALF : 2 * HALF] = low2[...]
    parcel[:, 2 * HALF :] = gate_query[...]


def later_kernel(rates, seg_column, seg_row, keys, values, outgoing, base_key, base_value, out, total):
    total[...] = base_value[...]
    for head in range(HEADS):
        begin, end = window(head)
        own = slice(head * KH, (head + 1) * KH)
        value = head_part(values, head, PIECE).astype(BF)
        tail = tail_of(rates[head], seg_column[...], seg_row[...])
        grad_key = base_key[:, own] + tail * product_right(value, outgoing[:, begin:end])
        out[:, own] = grad_key.astype(BF)
        total[:, begin:end] += jnp.where(inside(head, PIECE), tail * product(keys[:, own], outgoing[:, begin:end]), 0.0)
    out[:, HALF:] = total[...].astype(BF)


def first_back_kernel(
    gate_query, gate_query_theirs, key_value, key_value_theirs, query_weight, key_weight, value_weight, gate_weight,
    part, helped,
):
    both = jnp.concatenate([gate_query[...], gate_query_theirs[...]], 0)
    total = product_right(both[:, VPAD:], query_weight[...])
    total += product(both[:, :VW], gate_weight[...])
    both = jnp.concatenate([key_value[...], key_value_theirs[...]], 0)
    total += product_right(both[:, :HALF], key_weight[...])
    total += product(both[:, HALF : HALF + VW], value_weight[...])
    part[...] = total[:PIECE].astype(BF)
    helped[...] = total[PIECE:].astype(BF)


def last_kernel(
    shard, mine, theirs, helped, helped_other, normed, inverse, gain, grad_middle, vectors, out, vec_own, vec_oth
):
    grads = [
        mine[...].astype(F32) + theirs[...].astype(F32),
        helped[...].astype(F32) + helped_other[...].astype(F32),
    ]
    norms = [normed[:, :HALF], normed[:, HALF:]]
    for k, vec in enumerate((vec_own, vec_oth)):
        cut = slice(k * HALF, (k + 1) * HALF)
        rows = [jnp.sum(grads[k] * norms[k], 0, keepdims=True), jnp.sum(grads[k], 0, keepdims=True)]
        rows += [vectors[0:1, cut], vectors[1:2, cut], jnp.zeros((12, HALF), F32)]
        vec[...] = jnp.concatenate(rows, 0).astype(BF)
    back = norm_back(grads, own_first(shard[0], gain[...]), norms, inverse[:, :1])
    total = [grad_middle[:, :HALF] + back[0], grad_middle[:, HALF:] + back[1]]
    out[:, :HALF] = jnp.where(shard[0] == 0, total[0], total[1])
    out[:, HALF:] = jnp.where(shard[0] == 0, total[1], total[0])


def rows_of(core):
    column = lax.broadcasted_iota(jnp.int32, (HALF // 2, HALF), 1)
    row = lax.broadcasted_iota(jnp.int32, (HALF // 2, HALF), 0)
    source = (row // BLOCK * 2 + core) * BLOCK + row % BLOCK
    return (column == source).astype(F32).astype(BF)


def rows_kernel(core, *refs):
    count = (len(refs) - 2) // 2
    for chosen, out in ((core[0], refs[-2]), (1 - core[0], refs[-1])):
        pick = rows_of(chosen)
        for k in range(2 * count):
            out[:, k * PIECE : (k + 1) * PIECE] = product_right(pick, refs[k][...]).astype(BF)


def rows_more_kernel(core, low2, gb, sent, *refs):
    kept, gone, gate_query = refs[-3:]
    parts = [low2, sent.at[:, HALF : 2 * HALF], gb, sent.at[:, :HALF]]
    for chosen, out in ((core[0], kept), (1 - core[0], gone)):
        pick = rows_of(chosen)
        for k in range(4):
            out[:, k * PIECE : (k + 1) * PIECE] = product_right(pick, parts[k][...]).astype(BF)
    gate_query[...] = sent[:, 2 * HALF :]


def features_of(core, own, received):
    both = shape(HALF // 2, 2 * PIECE)
    kept, gone = run(rows_kernel, (both, both), [core], [own, received])
    return kept, core_swap(gone)


def all_tokens(array, other):
    return (array, other, core_swap(array), core_swap(other))


CHUNK = 896


def outer(features, groups, plan, chunk=CHUNK, vectors=None, core=None, later=()):
    steps = len(plan)
    flat = [a for kept, got, _ in features for a in (kept, got)]
    flat += [a for group in groups for a in group] + list(vectors or ())
    specs = []
    for _, _, block in features:
        specs += [pl.BlockSpec((HALF // 2, 2 * PIECE), lambda i, c, block=block: (0, block))] * 2
    for g in range(len(groups)):
        mine = [k for k in range(steps) if plan[k][1] == g]
        first, count, block = mine[0], len(mine), plan[mine[0]][2]
        assert mine == list(range(first, first + count))

        def place(i, c, first=first, count=count, block=block):
            return (0, block + jnp.clip(i - first, 0, count - 1))

        specs += [pl.BlockSpec((PIECE, chunk), place)] * 4
    specs += [pl.BlockSpec((16, HALF), lambda i, c: (0, 0))] * len(vectors or ())
    specs += [ANY] * len(later)
    flat += list(later)

    def chosen(step, column, choices):
        value = choices[plan[0][column]]
        for k in range(1, steps):
            if plan[k][column] != plan[k - 1][column]:
                value = jnp.where(step >= k, choices[plan[k][column]], value)
        return value

    def kernel(core, *refs):
        out = refs[-1]
        step = pl.program_id(0)
        count = 2 * len(features)
        left = [
            jnp.concatenate([refs[2 * k][...], refs[2 * k + 1][...]], 1) for k in range(len(features))
        ]
        right = [
            jnp.concatenate([refs[count + 4 * k + j][...] for j in range(4)], 0) for k in range(len(groups))
        ]
        out[...] = product(chosen(step, 0, left), chosen(step, 1, right)).astype(BF)
        if vectors is not None:

            @pl.when(step == steps - 1)
            def _():
                rows = refs[count + 4 * len(groups) :]
                total = (rows[0][...].astype(F32) + rows[1][...].astype(F32)) + (
                    rows[2][...].astype(F32) + rows[3][...].astype(F32)
                )
                column = lax.broadcasted_iota(jnp.int32, (16, 128), 1)
                row = lax.broadcasted_iota(jnp.int32, (16, 128), 0)
                shift = (column == row + 64).astype(F32).astype(BF)
                moved = product(product_right(rows_of(core[0]), total.astype(BF)).astype(BF), shift)
                out[:, chunk - 128 :] = (out[:, chunk - 128 :].astype(F32) + moved).astype(BF)

    if core is None:
        core = jnp.zeros((1,), jnp.int32)
    part = pl.pallas_call(
        kernel,
        out_shape=shape(HALF // 2, steps * chunk),
        grid_spec=pltpu.PrefetchScalarGridSpec(
            num_scalar_prefetch=1,
            grid=(steps,),
            in_specs=specs,
            out_specs=pl.BlockSpec((HALF // 2, chunk), lambda i, c: (0, i)),
        ),
        compiler_params=pltpu.CompilerParams(vmem_limit_bytes=56 * 1024 * 1024),
        cost_estimate=pl.CostEstimate(flops=0, bytes_accessed=0, transcendentals=0),
    )(core, *flat)
    return part.reshape(16, BLOCK, steps * chunk)


def sent(part):
    return lax.all_to_all(part, "ctx", 0, 0, axis_index_groups=PLANE, tiled=True)


def added(parts):
    return jnp.sum(parts.astype(F32), 0)


def body(
    tokens,
    segments,
    decay_rate,
    first_gain,
    first_bias,
    query_weight,
    key_weight,
    value_weight,
    gate_weight,
    out_weight,
    second_gain,
    second_bias,
    mlp_gate,
    mlp_up,
    mlp_down,
    upstream,
):
    shard = lax.axis_index("shard").astype(jnp.int32).reshape(1)
    ctx = lax.axis_index("ctx").astype(jnp.int32).reshape(1)
    core = ctx % 2
    tokens, upstream = tokens[0], upstream[0]
    value_turned, gate_turned, mlp_gate_turned, mlp_up_turned = value_weight.T, gate_weight.T, mlp_gate.T, mlp_up.T
    gain1, bias1, gain2, bias2 = first_gain[None], first_bias[None], second_gain[None], second_bias[None]
    seg = segments[0].astype(F32)
    seg_column, seg_row = seg[:, None], seg[None, :]
    weight = pltpu.VMEM((VW, HALF), BF)
    held = pltpu.VMEM((HALF, VPAD), BF)
    small = shape(PIECE, HALF)
    wide = shape(PIECE, WIDE)
    scale = shape(PIECE, 128, kind=F32)

    def dma(count):
        return pltpu.SemaphoreType.DMA((count,))

    normed1, inverse1, low1_own, low1_oth, packed = run(
        first_kernel,
        (shape(PIECE, WIDE, kind=F32), scale, small, small, shape(BLOCK, PACKED)),
        [ctx, shard],
        [tokens, gain1, bias1],
        [mlp_gate_turned, mlp_up_turned, out_weight],
        [pltpu.VMEM((GATHERED, VW, 128), BF), dma(GATHERED)],
    )
    low1_theirs = from_shard(low1_oth)
    packed = from_shard(after(packed, low1_theirs))
    theirs_key, theirs_value = run(
        help_kernel,
        (shape(PIECE, HALF, kind=F32), shape(PIECE, VW, kind=F32)),
        [],
        [low1_theirs, key_weight, value_turned],
    )
    helped_key, helped_value = half_from_shard(theirs_key), half_from_shard(theirs_value)
    theirs_query, theirs_gate = run(
        help_more_kernel,
        (shape(PIECE, HALF, kind=F32), shape(PIECE, VW, kind=F32)),
        [],
        [low1_theirs, query_weight, gate_turned],
    )
    helped_query, helped_gate = half_from_shard(theirs_query), half_from_shard(theirs_gate)
    base_query, base_key, base_value, base_gate = run(
        base_kernel,
        tuple(shape(PIECE, n, kind=F32) for n in (HALF, HALF, VW, VW)),
        [],
        [low1_own, query_weight, key_weight, value_turned, gate_turned],
        [theirs_key],
    )

    up_own, up_oth = run(turn_kernel, (small, small), [shard], [upstream])
    up_theirs = from_shard(up_oth)
    others = lax.all_gather(after(packed, theirs_value, up_theirs), "ctx", axis=0, tiled=True)


    def exchange(states, reverse, *before):
        mine = lax.all_to_all(states.reshape(NC, KH // NC, VPAD), "ctx", 0, 0, tiled=True)
        done = run(functools.partial(scan_kernel, reverse), shape(NC, KH // NC, VPAD), [decay_rate], [mine], before)
        return lax.all_to_all(done, "ctx", 0, 0, tiled=True).reshape(KH, VPAD), mine, done

    keys, values, local = run(
        local_kernel,
        (small, shape(PIECE, VPAD), shape(KH, VPAD)),
        [decay_rate],
        [seg_column, seg_row, base_key, base_value, helped_key, helped_value],
        [theirs_query],
        scratch=[pltpu.VMEM((KH, VPAD), F32)],
    )
    base_hidden, theirs_hidden = run(
        hidden_kernel,
        (shape(PIECE, VW, kind=F32), shape(PIECE, VW, kind=F32)),
        [],
        [up_own, up_theirs, mlp_down],
    )
    helped_hidden = half_from_shard(theirs_hidden)
    incoming, _, _ = exchange(local, False, helped_query, helped_gate, theirs_hidden)
    queries, inner, masked = run(
        inner_kernel,
        (small, shape(PIECE, VPAD, kind=F32), shape(HEADS, PIECE, PIECE)),
        [decay_rate],
        [seg_column, seg_row, base_query, helped_query, keys, values],
    )
    up_features = features_of(core, up_own, up_theirs)
    low1_features = features_of(core, low1_own, low1_theirs)
    gate_pre, grouped, scales, mixed, part = run(
        mix_kernel,
        (shape(PIECE, VW, kind=F32), shape(PIECE, VPAD, kind=F32), scale, shape(PIECE, VPAD), wide),
        [decay_rate],
        [seg_column, queries, inner, incoming, base_gate, helped_gate],
        [out_weight, others, helped_hidden],
        [pltpu.VMEM((PIECE, VPAD), F32), held, weight, dma(2)],
    )
    theirs = from_tp(part)
    middle, normed2, inverse2, low2_own, low2_oth, mlp_parts, part = run(
        mlp_kernel,
        (shape(PIECE, WIDE, kind=F32), shape(PIECE, WIDE, kind=F32), scale, small, small, shape(PIECE, 4 * VPAD), wide),
        [shard],
        [tokens, part, theirs, gain2, bias2, base_hidden, helped_hidden, mixed],
        [mlp_gate_turned, mlp_up_turned, others, up_features[1], low1_features[1]],
        [weight, weight, held, held, dma(4)],
    )
    theirs = from_tp(part)
    mlp_parts = after(mlp_parts, theirs)
    mlp_theirs = from_shard(mlp_parts)
    grad_middle, gb_own, gb_oth, vectors, grad_gate, grad_retained, term = run(
        unmix_kernel,
        (
            shape(PIECE, WIDE, kind=F32),
            small,
            small,
            shape(8, WIDE, kind=F32),
            shape(PIECE, VPAD),
            shape(PIECE, VPAD),
            shape(KH, VPAD),
        ),
        [shard, decay_rate],
        [part, theirs, normed2, inverse2, gain2, up_own, up_oth]
        + [seg_column, seg_row, queries, incoming, gate_pre, grouped, scales],
        [out_weight, others],
        [pltpu.VMEM((PIECE, VPAD), F32), pltpu.VMEM((KH, VPAD), F32), weight, held, dma(2)],
    )

    gate_query, parcel, base_key_grad, base_value_grad = run(
        back_kernel,
        (
            shape(PIECE, VPAD + HALF),
            shape(PIECE, 2 * HALF + VPAD + HALF),
            shape(PIECE, HALF, kind=F32),
            shape(PIECE, VPAD, kind=F32),
        ),
        [decay_rate],
        [seg_column, seg_row, queries, keys, values, masked, incoming, grad_retained, grad_gate, gb_oth, low2_oth],
    )
    parcel = from_shard(parcel)
    outgoing, _, scanned = exchange(term, True, gate_query)
    key_value = run(
        later_kernel,
        shape(PIECE, HALF + VPAD),
        [decay_rate],
        [seg_column, seg_row, keys, values, outgoing, base_key_grad, base_value_grad],
        scratch=[pltpu.VMEM((PIECE, VPAD), F32)],
    )
    key_value_theirs = from_shard(key_value)

    mlp_parts, mlp_theirs = hold((mlp_parts, mlp_theirs), scanned)
    both = shape(HALF // 2, 4 * PIECE)
    kept, gone, gate_query_theirs = run(
        rows_more_kernel, (both, both, shape(PIECE, VPAD + HALF)), [core], [low2_own, gb_own, parcel], [scanned]
    )
    got = core_swap(gone)
    early_part = outer(
        [(*up_features, 0), (kept, got, 0), (kept, got, 1)],
        [all_tokens(mlp_parts, mlp_theirs)],
        [(0, 0, 0), (1, 0, 1), (1, 0, 2), (2, 0, 3)],
        VPAD,
    )
    early = lax.psum_scatter(
        after(early_part, outgoing), "ctx", scatter_dimension=0, axis_index_groups=PLANE, tiled=False
    )
    early = early.astype(F32)
    gate_query, gate_query_theirs = hold((gate_query, gate_query_theirs), key_value)
    gate_query_parts = sent(
        outer(
            [(*low1_features, 0)],
            [all_tokens(gate_query, gate_query_theirs)],
            [(0, 0, 0), (0, 0, 1)],
            (VPAD + HALF) // 2,
        )
    )
    first_weights = [query_weight, key_weight, value_turned, gate_turned]
    part, helped = run(
        first_back_kernel,
        (small, small),
        [],
        [gate_query, gate_query_theirs, key_value, key_value_theirs] + first_weights,
    )
    tokens_grad, vec_own, vec_oth = run(
        last_kernel,
        (shape(PIECE, WIDE, kind=F32), shape(16, HALF), shape(16, HALF)),
        [shard],
        [part, from_tp(part), from_shard(helped), lax.ppermute(helped, ("shard", "tp"), SHARD_TP)]
        + [normed1, inverse1, gain1, grad_middle, vectors],
    )
    sums = (
        vec_own,
        from_shard(vec_oth),
        core_swap(vec_own),
        lax.ppermute(vec_oth, ("shard", "ctx"), SHARD_CORE),
    )
    key_value_parts = sent(
        outer(
            [(*low1_features, 0)],
            [all_tokens(key_value, key_value_theirs)],
            [(0, 0, 0), (0, 0, 1)],
            (HALF + VPAD) // 2,
            vectors=sums,
            core=core,
            later=(gate_query_parts,),
        )
    )

    part = run(down_kernel, shape(2 * PIECE, HALF), [], [mlp_parts, mlp_theirs, mlp_down])
    down_own, down_gone = run(
        down_sum_kernel, (shape(PIECE, HALF, kind=F32), small), [], [part, from_tp(part)]
    )
    layer_out = run(result_kernel, wide, [shard], [middle, down_own, from_shard(down_gone)])

    gate_query_sums, key_value_sums = added(gate_query_parts), added(key_value_parts)
    norms = key_value_sums[:, HALF + VW : HALF + VW + 4].T
    early = [early[:, k * VPAD : k * VPAD + VW] for k in range(4)]
    return (
        layer_out[None],
        tokens_grad[None],
        norms[0],
        norms[1],
        gate_query_sums[:, VPAD:],
        key_value_sums[:, :HALF],
        key_value_sums[:, HALF : HALF + VW],
        gate_query_sums[:, :VW],
        early[3].T,
        norms[2],
        norms[3],
        early[1],
        early[2],
        early[0].T,
    )


def solution(mesh):
    in_specs = (
        P("shard", "ctx", None),
        P("shard", "ctx"),
        P("tp"),
        P(),
        P(),
        P("shard", "tp"),
        P("shard", "tp"),
        P("shard", "tp"),
        P("shard", "tp"),
        P("tp", "shard"),
        P(),
        P(),
        P("shard", "tp"),
        P("shard", "tp"),
        P("tp", "shard"),
        P("shard", "ctx", None),
    )
    out_specs = (
        P("shard", "ctx", None),
        P("shard", "ctx", None),
        P(("shard", "ctx")),
        P(("shard", "ctx")),
        P(("shard", "ctx"), "tp"),
        P(("shard", "ctx"), "tp"),
        P(("shard", "ctx"), "tp"),
        P(("shard", "ctx"), "tp"),
        P("tp", ("shard", "ctx")),
        P(("shard", "ctx")),
        P(("shard", "ctx")),
        P(("shard", "ctx"), "tp"),
        P(("shard", "ctx"), "tp"),
        P("tp", ("shard", "ctx")),
    )
    return jax.shard_map(body, mesh=mesh, in_specs=in_specs, out_specs=out_specs, check_vma=False)
```

```python
import functools

import jax
import jax.numpy as jnp
from jax import lax
from jax.experimental import pallas as pl
from jax.experimental.pallas import tpu as pltpu
from jax.sharding import PartitionSpec as P

KH = 256
VH = 432
EPS = 1e-05
BF = jnp.bfloat16
F32 = jnp.float32
F16 = jnp.float16
NC = 32
BLOCK = 32
HALF = 1024
VW = 1728
VPAD = 1792
HEADS = 4
PIECE = 128
QKV = 2 * HALF + VW
GATHERED = 3
PACKED = GATHERED * VPAD
WIDE = 2048

SWAP = [(0, 1), (1, 0)]
CORE = [(index, index ^ 1) for index in range(NC)]
SHARD_TP = [(0, 3), (1, 2), (2, 1), (3, 0)]
SHARD_CORE = [(index, (index ^ 1) ^ NC) for index in range(2 * NC)]
PLANE = [[2 * chip + core for chip in range(16)] for core in range(2)]
ANY = pl.BlockSpec(memory_space=pl.ANY)
SMEM = pl.BlockSpec(memory_space=pltpu.SMEM)


def product(left, right):
    return jnp.dot(left, right, preferred_element_type=F32)


def product_left(left, right):
    return lax.dot_general(left, right, (((0,), (0,)), ((), ())), preferred_element_type=F32)


def product_right(left, right):
    return lax.dot_general(left, right, (((1,), (1,)), ((), ())), preferred_element_type=F32)


def from_shard(part):
    return lax.ppermute(part, "shard", SWAP)


def half_from_shard(part):
    return lax.ppermute(part.astype(F16), "shard", SWAP).astype(F32)


def from_tp(part):
    return lax.ppermute(part, "tp", SWAP)


def core_swap(part):
    return lax.ppermute(part, "ctx", CORE)


def shape(*dims, kind=BF):
    return jax.ShapeDtypeStruct(dims, kind)


def whole(array):
    return pl.BlockSpec(array.shape, lambda i, rank=len(array.shape): (0,) * rank)


def run(kernel, outs, scalars, blocks, far=(), scratch=(), flops=0):
    single = not isinstance(outs, tuple)
    outs = (outs,) if single else outs
    got = pl.pallas_call(
        kernel,
        out_shape=outs,
        grid=(1,),
        in_specs=[SMEM] * len(scalars) + [whole(a) for a in blocks] + [ANY] * len(far),
        out_specs=tuple(whole(a) for a in outs),
        scratch_shapes=list(scratch),
        compiler_params=pltpu.CompilerParams(vmem_limit_bytes=56 * 1024 * 1024),
        cost_estimate=pl.CostEstimate(flops=flops, bytes_accessed=0, transcendentals=0),
    )(*scalars, *blocks, *far)
    return got[0] if single else got


def hold(arrays, *others):
    count = len(arrays)
    return pl.pallas_call(
        lambda *refs: None,
        out_shape=tuple(shape(*a.shape, kind=a.dtype) for a in arrays),
        in_specs=[ANY] * (count + len(others)),
        out_specs=(ANY,) * count,
        input_output_aliases={k: k for k in range(count)},
        cost_estimate=pl.CostEstimate(flops=0, bytes_accessed=0, transcendentals=0),
    )(*arrays, *others)


def after(array, *others):
    return hold((array,), *others)[0]


def fetch(sources, holders, semaphores):
    copies = [pltpu.make_async_copy(src, dst, semaphores.at[k]) for k, (src, dst) in enumerate(zip(sources, holders))]
    for copy in copies:
        copy.start()
    return copies


def part_of(others, k):
    return others.at[:, k * VPAD : (k + 1) * VPAD]


def own_first(shard, array):
    a, b = array[:, :HALF], array[:, HALF:]
    return jnp.where(shard == 0, a, b), jnp.where(shard == 0, b, a)


def normed_of(own, oth):
    mean = (jnp.sum(own, 1, keepdims=True) + jnp.sum(oth, 1, keepdims=True)) / WIDE
    own, oth = own - mean, oth - mean
    var = (jnp.sum(own * own, 1, keepdims=True) + jnp.sum(oth * oth, 1, keepdims=True)) / WIDE
    inverse = lax.rsqrt(var + EPS)
    return own * inverse, oth * inverse, inverse


def norm_back(grads, gains, normed, inverse):
    grads = [grad * gain for grad, gain in zip(grads, gains)]
    mean = sum(jnp.sum(g, 1, keepdims=True) for g in grads) / WIDE
    slant = sum(jnp.sum(g * n, 1, keepdims=True) for g, n in zip(grads, normed)) / WIDE
    return [inverse * (g - mean - n * slant) for g, n in zip(grads, normed)]


def first_kernel(place, shard, tokens, gain, bias, *refs):
    weights, (normed, inverse, low_own, low_oth, packed, columns, semaphores) = refs[:GATHERED], refs[GATHERED:]
    begin = pl.multiple_of(place[0] // 4 * 128, 128)
    copies = fetch([w.at[:, pl.ds(begin, 128)] for w in weights], [columns.at[k] for k in range(GATHERED)], semaphores)
    own, oth = own_first(shard[0], tokens[...].astype(F32))
    own, oth, scale = normed_of(own, oth)
    gains, biases = own_first(shard[0], gain[...]), own_first(shard[0], bias[...])
    normed[:, :HALF] = own
    normed[:, HALF:] = oth
    inverse[...] = jnp.broadcast_to(scale, inverse.shape)
    low_own[...] = (own * gains[0] + biases[0]).astype(BF)
    low_oth[...] = (oth * gains[1] + biases[1]).astype(BF)
    packed[...] = jnp.zeros_like(packed)
    column = lax.broadcasted_iota(jnp.int32, (BLOCK, 128), 1)
    wanted = lax.broadcasted_iota(jnp.int32, (BLOCK, 128), 0) + (place[0] % 4) * BLOCK
    chosen = (column == wanted).astype(F32).astype(BF)
    for k in range(GATHERED):
        copies[k].wait()
        packed[:, k * VPAD : k * VPAD + VW] = product_right(chosen, columns[k]).astype(BF)


def turn_kernel(shard, array, own, oth):
    own[...], oth[...] = own_first(shard[0], array[...])


def help_kernel(low, key_weight, value_weight, key, value):
    key[...] = product(low[...], key_weight[...])
    value[...] = product_right(low[...], value_weight[...])


def help_more_kernel(low, query_weight, gate_weight, query, gate):
    query[...] = product(low[...], query_weight[...])
    gate[...] = product_right(low[...], gate_weight[...])


def base_kernel(low, query_weight, key_weight, value_weight, gate_weight, _, query, key, value, gate):
    query[...] = product(low[...], query_weight[...])
    key[...] = product(low[...], key_weight[...])
    value[...] = product_right(low[...], value_weight[...])
    gate[...] = product_right(low[...], gate_weight[...])


def hidden_kernel(own, theirs, weight, base, helped):
    both = jnp.concatenate([own[...], theirs[...]], 0)
    total = product_right(both, weight[...])
    base[...] = total[:PIECE]
    helped[...] = total[PIECE:]


def window(head):
    begin = head * VH // 128 * 128
    end = -(-(head + 1) * VH // 128) * 128
    return begin, end


def inside(head, rows):
    begin, end = window(head)
    column = lax.broadcasted_iota(jnp.int32, (rows, end - begin), 1) + begin
    return (column >= head * VH) & (column < (head + 1) * VH)


def head_part(ref, head, rows):
    begin, end = window(head)
    return jnp.where(inside(head, rows), ref[:, begin:end].astype(F32), 0.0)


def decay_of(rate, seg_column, seg_row):
    down = lax.broadcasted_iota(jnp.int32, (PIECE, PIECE), 0) - lax.broadcasted_iota(jnp.int32, (PIECE, PIECE), 1)
    near = jnp.exp(-rate * jnp.maximum(down, 0).astype(F32))
    return jnp.where((down >= 0) & (seg_column == seg_row), near, 0.0)


def tail_of(rate, seg_column, seg_row):
    left = (PIECE - 1 - lax.broadcasted_iota(jnp.int32, (PIECE, 1), 0)).astype(F32)
    return jnp.where(seg_column == seg_row[:, PIECE - 1 :], jnp.exp(-rate * left), 0.0)


def reach_of(rate, seg_column, before):
    passed = (lax.broadcasted_iota(jnp.int32, (PIECE, 1), 0) + 1).astype(F32)
    return jnp.where(seg_column == before, jnp.exp(-rate * passed), 0.0)


def with_marks(total, seg_row):
    column = lax.broadcasted_iota(jnp.int32, total.shape, 1)
    marked = jnp.where(column == VW, seg_row[:, :1], jnp.where(column == VW + 1, seg_row[:, PIECE - 1 :], 0.0))
    return jnp.where(column < VW, total, marked).astype(BF)


def mark(states, offset):
    column = lax.broadcasted_iota(jnp.int32, (states.shape[0], 128), 1)
    return jnp.sum(jnp.where(column == VW - (VPAD - 128) + offset, states[:, VPAD - 128 :], 0.0), 1, keepdims=True)


def local_kernel(rates, seg_column, seg_row, base_key, base_value, helped_key, helped_value, _, keys, values, local, total):
    keys[...] = (base_key[...] + helped_key[...].astype(F32)).astype(BF)
    values[:, :VW] = (base_value[...] + helped_value[...].astype(F32)).astype(BF)
    values[:, VW:] = jnp.zeros((PIECE, VPAD - VW), BF)
    total[...] = jnp.zeros_like(total)
    for head in range(HEADS):
        begin, end = window(head)
        own = slice(head * KH, (head + 1) * KH)
        value = head_part(values, head, PIECE).astype(BF)
        key_tail = (keys[:, own].astype(F32) * tail_of(rates[head], seg_column[...], seg_row[...])).astype(BF)
        total[:, begin:end] += product_left(key_tail, value)
    local[...] = with_marks(total[...], seg_row[...])


def inner_kernel(rates, seg_column, seg_row, base_query, helped_query, keys, values, queries, inner, masked):
    queries[...] = (base_query[...] + helped_query[...].astype(F32)).astype(BF)
    inner[...] = jnp.zeros_like(inner)
    for head in range(HEADS):
        begin, end = window(head)
        own = slice(head * KH, (head + 1) * KH)
        scores = product_right(queries[:, own], keys[:, own])
        kept = (scores * decay_of(rates[head], seg_column[...], seg_row[...])).astype(BF)
        masked[head] = kept
        inner[:, begin:end] += product(kept, head_part(values, head, PIECE).astype(BF))


def scan_kernel(reverse, rates, states, *refs):
    out = refs[-1]
    column = lax.broadcasted_iota(jnp.int32, (8, VPAD), 1)
    rate = jnp.full((8, VPAD), rates[HEADS - 1], F32)
    for head in range(HEADS - 1):
        rate = jnp.where((column >= head * VH) & (column < (head + 1) * VH), rates[head], rate)
    factor = jnp.exp(-rate * PIECE)
    edges = [states[p, :, VPAD - 128 :].astype(F32) for p in range(NC)]

    def mark_of(p, offset):
        lane = lax.broadcasted_iota(jnp.int32, (8, 128), 1)
        return jnp.sum(jnp.where(lane == VW - (VPAD - 128) + offset, edges[p], 0.0), 1, keepdims=True)

    firsts = [mark_of(p, 0) for p in range(NC)]
    lasts = [mark_of(p, 1) for p in range(NC)]
    befores = [jnp.full((8, 1), -1.0, F32)] + lasts[:-1]
    carry = jnp.zeros((8, VPAD), F32)
    for k in range(NC):
        p = NC - 1 - k if reverse else k
        out[p] = jnp.where(column < VW, carry, befores[p]).astype(BF)
        keep = jnp.where((firsts[p] == lasts[p]) & (firsts[p] == befores[p]), factor, 0.0)
        carry = states[p].astype(F32) + keep * carry


def mix_kernel(
    rates, seg_column, queries, inner, incoming, base_gate, helped_gate, out_weight, others, _,
    gate, grouped, inverse, mixed, part, total, held, near, semaphores,
):
    copies = fetch([out_weight, part_of(others, 2)], [near, held], semaphores)
    gate[...] = base_gate[...] + helped_gate[...].astype(F32)
    before = mark(incoming[:16].astype(F32), 0)[:1]
    total[...] = inner[...]
    for head in range(HEADS):
        begin, end = window(head)
        own = slice(head * KH, (head + 1) * KH)
        across = product(queries[:, own], incoming[:, begin:end])
        total[:, begin:end] += jnp.where(
            inside(head, PIECE), reach_of(rates[head], seg_column[...], before) * across, 0.0
        )
    lane = lax.broadcasted_iota(jnp.int32, (PIECE, 128), 1)
    scales = jnp.zeros((PIECE, 128), F32)
    grouped[...] = jnp.zeros_like(grouped)
    for head in range(HEADS):
        begin, end = window(head)
        here = inside(head, PIECE)
        retained = jnp.where(here, total[:, begin:end], 0.0)
        center = jnp.where(here, retained - jnp.sum(retained, 1, keepdims=True) / VH, 0.0)
        scale = lax.rsqrt(jnp.sum(center * center, 1, keepdims=True) / VH + EPS)
        grouped[:, begin:end] += center * scale
        scales = jnp.where(lane == head, scale, scales)
    inverse[...] = scales
    mixed[:, :VW] = (jax.nn.silu(gate[...]) * grouped[:, :VW]).astype(BF)
    mixed[:, VW:] = jnp.zeros((PIECE, VPAD - VW), BF)
    copies[0].wait()
    part[:, :HALF] = product(mixed[:, :VW], near[...]).astype(BF)
    copies[1].wait()
    part[:, HALF:] = product_right(mixed[...], held[...]).astype(BF)


def mlp_kernel(
    shard, tokens, mine, theirs, gain, bias, base_hidden, helped_hidden, gate_weight, up_weight, others, _up, _low,
    middle, normed, inverse, low_own, grads, part,
    near_gate, near_up, far_gate, far_up, semaphores,
):
    copies = fetch(
        [gate_weight, part_of(others, 0), up_weight, part_of(others, 1)],
        [near_gate, far_gate, near_up, far_up],
        semaphores,
    )
    own, oth = own_first(shard[0], tokens[...].astype(F32))
    own = own + (mine[:, :HALF].astype(F32) + theirs[:, :HALF].astype(F32))
    oth = oth + (mine[:, HALF:].astype(F32) + theirs[:, HALF:].astype(F32))
    middle[:, :HALF] = own
    middle[:, HALF:] = oth
    own, oth, scale = normed_of(own, oth)
    gains, biases = own_first(shard[0], gain[...]), own_first(shard[0], bias[...])
    normed[:, :HALF] = own
    normed[:, HALF:] = oth
    inverse[...] = jnp.broadcast_to(scale, inverse.shape)
    low_own[...] = (own * gains[0] + biases[0]).astype(BF)
    low_oth = (oth * gains[1] + biases[1]).astype(BF)
    grads[:, 3 * VPAD :] = low_oth
    copies[0].wait()
    up_gate = product_right(low_own[...], near_gate[...])
    copies[1].wait()
    up_gate += product(low_oth, far_gate[:, :VW])
    copies[2].wait()
    up_vals = product_right(low_own[...], near_up[...])
    copies[3].wait()
    up_vals += product(low_oth, far_up[:, :VW])
    grad_hidden = base_hidden[...] + helped_hidden[...].astype(F32)
    sigma = jax.nn.sigmoid(up_gate)
    silu = up_gate * sigma
    none = jnp.zeros((PIECE, VPAD - VW), BF)
    for k, array in enumerate(
        (silu * up_vals, grad_hidden * up_vals * (sigma * (1.0 + up_gate * (1.0 - sigma))), grad_hidden * silu)
    ):
        grads[:, k * VPAD : k * VPAD + VW] = array.astype(BF)
        grads[:, k * VPAD + VW : (k + 1) * VPAD] = none
    total = product(grads[:, VPAD : VPAD + VW], near_gate[...])
    total += product(grads[:, 2 * VPAD : 2 * VPAD + VW], near_up[...])
    part[:, :HALF] = total.astype(BF)
    total = product_right(grads[:, VPAD : 2 * VPAD], far_gate[...])
    total += product_right(grads[:, 2 * VPAD : 3 * VPAD], far_up[...])
    part[:, HALF:] = total.astype(BF)


def down_kernel(own, theirs, weight, part):
    both = jnp.concatenate([own[:, :VW], theirs[:, :VW]], 0)
    part[...] = product(both, weight[...]).astype(BF)


def down_sum_kernel(mine, theirs, own, gone):
    own[...] = mine[:PIECE].astype(F32) + theirs[:PIECE].astype(F32)
    gone[...] = (mine[PIECE:].astype(F32) + theirs[PIECE:].astype(F32)).astype(BF)


def result_kernel(shard, middle, own, oth, out):
    total = [middle[:, :HALF] + own[...], middle[:, HALF:] + oth[...].astype(F32)]
    out[:, :HALF] = jnp.where(shard[0] == 0, total[0], total[1]).astype(BF)
    out[:, HALF:] = jnp.where(shard[0] == 0, total[1], total[0]).astype(BF)


def unmix_kernel(
    shard, rates, mine, theirs, normed, inverse, gain, up_own, up_oth, seg_column, seg_row, queries, incoming, gate,
    grouped, scales, out_weight, others,
    grad_middle, branch_own, branch_oth, vectors, grad_gate, grad_retained, term,
    held, total, near, far, semaphores,
):
    copies = fetch([out_weight, part_of(others, 2)], [near, far], semaphores)
    grads = [mine[:, cut].astype(F32) + theirs[:, cut].astype(F32) for cut in (slice(0, HALF), slice(HALF, WIDE))]
    norms = [normed[:, :HALF], normed[:, HALF:]]
    vectors[...] = jnp.zeros_like(vectors)
    for k in range(2):
        cut = slice(k * HALF, (k + 1) * HALF)
        vectors[0:1, cut] = jnp.sum(grads[k] * norms[k], 0, keepdims=True)
        vectors[1:2, cut] = jnp.sum(grads[k], 0, keepdims=True)
    back = norm_back(grads, own_first(shard[0], gain[...]), norms, inverse[:, :1])
    own, oth = up_own[...].astype(F32) + back[0], up_oth[...].astype(F32) + back[1]
    grad_middle[:, :HALF] = own
    grad_middle[:, HALF:] = oth
    branch_own[...] = own.astype(BF)
    branch_oth[...] = oth.astype(BF)
    before = mark(incoming[:16].astype(F32), 0)[:1]
    sigma = jax.nn.sigmoid(gate[...])
    copies[0].wait()
    grad_mixed = product_right(branch_own[...], near[...])
    copies[1].wait()
    grad_mixed += product(branch_oth[...], far[:, :VW])
    slope = sigma * (1.0 + gate[...] * (1.0 - sigma))
    none = jnp.zeros((PIECE, VPAD - VW), F32)
    grad_gate[:, :VW] = (grad_mixed * grouped[:, :VW] * slope).astype(BF)
    grad_gate[:, VW:] = none.astype(BF)
    held[:, :VW] = grad_mixed * (gate[...] * sigma)
    held[:, VW:] = none
    lane = lax.broadcasted_iota(jnp.int32, (PIECE, 128), 1)
    total[...] = jnp.zeros_like(total)
    for head in range(HEADS):
        begin, end = window(head)
        here = inside(head, PIECE)
        grad = head_part(held, head, PIECE)
        group = head_part(grouped, head, PIECE)
        scale = jnp.sum(jnp.where(lane == head, scales[...], 0.0), 1, keepdims=True)
        back = grad - jnp.sum(grad, 1, keepdims=True) / VH - group * (jnp.sum(grad * group, 1, keepdims=True) / VH)
        total[:PIECE, begin:end] += jnp.where(here, scale * back, 0.0)
    grad_retained[...] = total[:PIECE].astype(BF)
    total[...] = jnp.zeros_like(total)
    for head in range(HEADS):
        begin, end = window(head)
        own = slice(head * KH, (head + 1) * KH)
        reached = reach_of(rates[head], seg_column[...], before) * head_part(grad_retained, head, PIECE)
        total[:, begin:end] += product_left(queries[:, own], reached.astype(BF))
    term[...] = with_marks(total[...], seg_row[...])


def back_kernel(
    rates, seg_column, seg_row, queries, keys, values, masked, incoming, grad_retained, grad_gate, gb, mixed,
    gate_query, parcel, base_key, base_value,
):
    before = mark(incoming[:16].astype(F32), 0)[:1]
    gate_query[:, :VPAD] = grad_gate[...]
    base_value[...] = jnp.zeros_like(base_value)
    for head in range(HEADS):
        rate = rates[head]
        begin, end = window(head)
        own = slice(head * KH, (head + 1) * KH)
        value = head_part(values, head, PIECE).astype(BF)
        grad = head_part(grad_retained, head, PIECE).astype(BF)
        decay = decay_of(rate, seg_column[...], seg_row[...])
        reach = reach_of(rate, seg_column[...], before)
        grad_scores = (product_right(grad, value) * decay).astype(BF)
        grad_query = product(grad_scores, keys[:, own])
        grad_query += reach * product_right(grad, incoming[:, begin:end])
        gate_query[:, VPAD + head * KH : VPAD + (head + 1) * KH] = grad_query.astype(BF)
        base_key[:, own] = product_left(grad_scores, queries[:, own])
        base_value[:, begin:end] += product_left(masked[head], grad)
    parcel[:, :VPAD] = mixed[...]
    parcel[:, VPAD:] = gb[...]


def later_kernel(rates, seg_column, seg_row, keys, values, outgoing, base_key, base_value, _theirs, _early, out, total):
    total[...] = base_value[...]
    for head in range(HEADS):
        begin, end = window(head)
        own = slice(head * KH, (head + 1) * KH)
        value = head_part(values, head, PIECE).astype(BF)
        tail = tail_of(rates[head], seg_column[...], seg_row[...])
        grad_key = base_key[:, own] + tail * product_right(value, outgoing[:, begin:end])
        out[:, own] = grad_key.astype(BF)
        total[:, begin:end] += jnp.where(inside(head, PIECE), tail * product(keys[:, own], outgoing[:, begin:end]), 0.0)
    out[:, HALF:] = total[...].astype(BF)


def first_back_kernel(
    gate_query, gate_query_theirs, key_value, key_value_theirs, query_weight, key_weight, value_weight, gate_weight,
    part, helped,
):
    both = jnp.concatenate([gate_query[...], gate_query_theirs[...]], 0)
    total = product_right(both[:, VPAD : VPAD + HALF], query_weight[...])
    total += product(both[:, :VW], gate_weight[...])
    both = jnp.concatenate([key_value[...], key_value_theirs[...]], 0)
    total += product_right(both[:, :HALF], key_weight[...])
    total += product(both[:, HALF : HALF + VW], value_weight[...])
    part[...] = total[:PIECE].astype(BF)
    helped[...] = total[PIECE:].astype(BF)


def last_kernel(
    shard, mine, theirs, helped, helped_other, normed, inverse, gain, grad_middle, vectors, out, vec_own, vec_oth
):
    grads = [
        mine[...].astype(F32) + theirs[...].astype(F32),
        helped[...].astype(F32) + helped_other[...].astype(F32),
    ]
    norms = [normed[:, :HALF], normed[:, HALF:]]
    for k, vec in enumerate((vec_own, vec_oth)):
        cut = slice(k * HALF, (k + 1) * HALF)
        rows = [jnp.sum(grads[k] * norms[k], 0, keepdims=True), jnp.sum(grads[k], 0, keepdims=True)]
        rows += [vectors[0:1, cut], vectors[1:2, cut], jnp.zeros((12, HALF), F32)]
        vec[...] = jnp.concatenate(rows, 0).astype(BF)
    back = norm_back(grads, own_first(shard[0], gain[...]), norms, inverse[:, :1])
    total = [grad_middle[:, :HALF] + back[0], grad_middle[:, HALF:] + back[1]]
    out[:, :HALF] = jnp.where(shard[0] == 0, total[0], total[1])
    out[:, HALF:] = jnp.where(shard[0] == 0, total[1], total[0])


def rows_of(core):
    column = lax.broadcasted_iota(jnp.int32, (HALF // 2, HALF), 1)
    row = lax.broadcasted_iota(jnp.int32, (HALF // 2, HALF), 0)
    source = (row // BLOCK * 2 + core) * BLOCK + row % BLOCK
    return (column == source).astype(F32).astype(BF)


def rows_kernel(core, *refs):
    count = (len(refs) - 2) // 2
    for chosen, out in ((core[0], refs[-2]), (1 - core[0], refs[-1])):
        pick = rows_of(chosen)
        for k in range(2 * count):
            out[:, k * PIECE : (k + 1) * PIECE] = product_right(pick, refs[k][...]).astype(BF)


def rows_cut_kernel(start, core, own, sent, *refs):
    kept, gone = refs[-2:]
    for chosen, out in ((core[0], kept), (1 - core[0], gone)):
        pick = rows_of(chosen)
        out[:, :PIECE] = product_right(pick, own[...]).astype(BF)
        out[:, PIECE:] = product_right(pick, sent[:, start : start + HALF]).astype(BF)


def features_of(core, own, received):
    both = shape(HALF // 2, 2 * PIECE)
    kept, gone = run(rows_kernel, (both, both), [core], [own, received])
    return kept, core_swap(gone)


def features_in(core, own, sent, start, *later):
    both = shape(HALF // 2, 2 * PIECE)
    kept, gone = run(functools.partial(rows_cut_kernel, start), (both, both), [core], [own, sent], later)
    return kept, core_swap(gone)


def all_tokens(array, other):
    return (array, other, core_swap(array), core_swap(other))


def outer(features, groups, plan, chunk, width, vectors=None, core=None, later=(), flops=0):
    steps = len(plan)
    flat = [a for pair in features for a in pair]
    flat += [a for group in groups for a in group] + list(vectors or ())
    specs = [pl.BlockSpec((HALF // 2, 2 * PIECE), lambda i, c: (0, 0))] * (2 * len(features))
    for g in range(len(groups)):
        mine = [k for k in range(steps) if plan[k][1] == g]
        first, count, block = mine[0], len(mine), plan[mine[0]][2]
        assert mine == list(range(first, first + count))

        def place(i, c, first=first, count=count, block=block):
            return (0, block + jnp.clip(i - first, 0, count - 1))

        specs += [pl.BlockSpec((PIECE, chunk), place)] * 4
    specs += [pl.BlockSpec((16, HALF), lambda i, c: (0, 0))] * len(vectors or ())
    specs += [ANY] * len(later)
    flat += list(later)

    def chosen(step, column, choices):
        value = choices[plan[0][column]]
        for k in range(1, steps):
            if plan[k][column] != plan[k - 1][column]:
                value = jnp.where(step >= k, choices[plan[k][column]], value)
        return value

    def kernel(core, *refs):
        out = refs[-1]
        step = pl.program_id(0)
        count = 2 * len(features)
        left = [
            jnp.concatenate([refs[2 * k][...], refs[2 * k + 1][...]], 1) for k in range(len(features))
        ]
        right = [
            jnp.concatenate([refs[count + 4 * k + j][...] for j in range(4)], 0) for k in range(len(groups))
        ]
        out[...] = product(chosen(step, 0, left), chosen(step, 1, right)).astype(BF)
        if vectors is not None:

            @pl.when(step == steps - 1)
            def _():
                rows = refs[count + 4 * len(groups) :]
                total = (rows[0][...].astype(F32) + rows[1][...].astype(F32)) + (
                    rows[2][...].astype(F32) + rows[3][...].astype(F32)
                )
                column = lax.broadcasted_iota(jnp.int32, (16, 128), 1)
                row = lax.broadcasted_iota(jnp.int32, (16, 128), 0)
                shift = (column == row + 64).astype(F32).astype(BF)
                moved = product(product_right(rows_of(core[0]), total.astype(BF)).astype(BF), shift)
                out[:, chunk - 128 :] = (out[:, chunk - 128 :].astype(F32) + moved).astype(BF)

    if core is None:
        core = jnp.zeros((1,), jnp.int32)
    part = pl.pallas_call(
        kernel,
        out_shape=shape(HALF // 2, width),
        grid_spec=pltpu.PrefetchScalarGridSpec(
            num_scalar_prefetch=1,
            grid=(steps,),
            in_specs=specs,
            out_specs=pl.BlockSpec((HALF // 2, chunk), lambda i, c: (0, i)),
        ),
        compiler_params=pltpu.CompilerParams(vmem_limit_bytes=56 * 1024 * 1024),
        cost_estimate=pl.CostEstimate(flops=flops, bytes_accessed=0, transcendentals=0),
    )(core, *flat)
    return part.reshape(16, BLOCK, width)


def sum_kernel(parts, key, value, norms):
    total = parts[0].astype(F32)
    for k in range(1, 16):
        total += parts[k].astype(F32)
    key[...] = total[:, :HALF]
    value[...] = total[:, HALF : HALF + VW]
    norms[...] = total[:, HALF + VPAD - 128 :]


def sent(part):
    return lax.all_to_all(part, "ctx", 0, 0, axis_index_groups=PLANE, tiled=True)


def added(parts):
    return jnp.sum(parts.astype(F32), 0)


def body(
    tokens,
    segments,
    decay_rate,
    first_gain,
    first_bias,
    query_weight,
    key_weight,
    value_weight,
    gate_weight,
    out_weight,
    second_gain,
    second_bias,
    mlp_gate,
    mlp_up,
    mlp_down,
    upstream,
):
    shard = lax.axis_index("shard").astype(jnp.int32).reshape(1)
    ctx = lax.axis_index("ctx").astype(jnp.int32).reshape(1)
    core = ctx % 2
    tokens, upstream = tokens[0], upstream[0]
    value_turned, gate_turned, mlp_gate_turned, mlp_up_turned = value_weight.T, gate_weight.T, mlp_gate.T, mlp_up.T
    gain1, bias1, gain2, bias2 = first_gain[None], first_bias[None], second_gain[None], second_bias[None]
    seg = segments[0].astype(F32)
    seg_column, seg_row = seg[:, None], seg[None, :]
    weight = pltpu.VMEM((VW, HALF), BF)
    held = pltpu.VMEM((HALF, VPAD), BF)
    small = shape(PIECE, HALF)
    wide = shape(PIECE, WIDE)
    scale = shape(PIECE, 128, kind=F32)

    def dma(count):
        return pltpu.SemaphoreType.DMA((count,))

    normed1, inverse1, low1_own, low1_oth, packed = run(
        first_kernel,
        (shape(PIECE, WIDE, kind=F32), scale, small, small, shape(BLOCK, PACKED)),
        [ctx, shard],
        [tokens, gain1, bias1],
        [mlp_gate_turned, mlp_up_turned, out_weight],
        [pltpu.VMEM((GATHERED, VW, 128), BF), dma(GATHERED)],
    )
    low1_theirs = from_shard(low1_oth)
    packed = from_shard(after(packed, low1_theirs))
    theirs_key, theirs_value = run(
        help_kernel,
        (shape(PIECE, HALF, kind=F32), shape(PIECE, VW, kind=F32)),
        [],
        [low1_theirs, key_weight, value_turned],
    )
    helped_key, helped_value = half_from_shard(theirs_key), half_from_shard(theirs_value)
    theirs_query, theirs_gate = run(
        help_more_kernel,
        (shape(PIECE, HALF, kind=F32), shape(PIECE, VW, kind=F32)),
        [],
        [low1_theirs, query_weight, gate_turned],
    )
    helped_query, helped_gate = half_from_shard(theirs_query), half_from_shard(theirs_gate)
    base_query, base_key, base_value, base_gate = run(
        base_kernel,
        tuple(shape(PIECE, n, kind=F32) for n in (HALF, HALF, VW, VW)),
        [],
        [low1_own, query_weight, key_weight, value_turned, gate_turned],
        [theirs_key],
    )

    up_own, up_oth = run(turn_kernel, (small, small), [shard], [upstream])
    up_theirs = from_shard(up_oth)
    others = lax.all_gather(after(packed, theirs_value, up_theirs), "ctx", axis=0, tiled=True)


    def exchange(states, reverse, *before):
        mine = lax.all_to_all(states.reshape(NC, KH // NC, VPAD), "ctx", 0, 0, tiled=True)
        done = run(functools.partial(scan_kernel, reverse), shape(NC, KH // NC, VPAD), [decay_rate], [mine], before)
        return lax.all_to_all(done, "ctx", 0, 0, tiled=True).reshape(KH, VPAD), mine, done

    keys, values, local = run(
        local_kernel,
        (small, shape(PIECE, VPAD), shape(KH, VPAD)),
        [decay_rate],
        [seg_column, seg_row, base_key, base_value, helped_key, helped_value],
        [theirs_query],
        scratch=[pltpu.VMEM((KH, VPAD), F32)],
    )
    base_hidden, theirs_hidden = run(
        hidden_kernel,
        (shape(PIECE, VW, kind=F32), shape(PIECE, VW, kind=F32)),
        [],
        [up_own, up_theirs, mlp_down],
    )
    helped_hidden = half_from_shard(theirs_hidden)
    incoming, _, _ = exchange(local, False, helped_query, helped_gate, theirs_hidden)
    queries, inner, masked = run(
        inner_kernel,
        (small, shape(PIECE, VPAD, kind=F32), shape(HEADS, PIECE, PIECE)),
        [decay_rate],
        [seg_column, seg_row, base_query, helped_query, keys, values],
    )
    up_features = features_of(core, up_own, up_theirs)
    low1_features = features_of(core, low1_own, low1_theirs)
    gate_pre, grouped, scales, mixed, part = run(
        mix_kernel,
        (shape(PIECE, VW, kind=F32), shape(PIECE, VPAD, kind=F32), scale, shape(PIECE, VPAD), wide),
        [decay_rate],
        [seg_column, queries, inner, incoming, base_gate, helped_gate],
        [out_weight, others, helped_hidden],
        [pltpu.VMEM((PIECE, VPAD), F32), held, weight, dma(2)],
    )
    theirs = from_tp(part)
    middle, normed2, inverse2, low2_own, mlp_parts, part = run(
        mlp_kernel,
        (shape(PIECE, WIDE, kind=F32), shape(PIECE, WIDE, kind=F32), scale, small, shape(PIECE, 3 * VPAD + HALF), wide),
        [shard],
        [tokens, part, theirs, gain2, bias2, base_hidden, helped_hidden],
        [mlp_gate_turned, mlp_up_turned, others, up_features[1], low1_features[1]],
        [weight, weight, held, held, dma(4)],
    )
    theirs = from_tp(part)
    mlp_parts = after(mlp_parts, theirs)
    mlp_theirs = from_shard(mlp_parts)
    grad_middle, gb_own, gb_oth, vectors, grad_gate, grad_retained, term = run(
        unmix_kernel,
        (
            shape(PIECE, WIDE, kind=F32),
            small,
            small,
            shape(8, WIDE, kind=F32),
            shape(PIECE, VPAD),
            shape(PIECE, VPAD),
            shape(KH, VPAD),
        ),
        [shard, decay_rate],
        [part, theirs, normed2, inverse2, gain2, up_own, up_oth]
        + [seg_column, seg_row, queries, incoming, gate_pre, grouped, scales],
        [out_weight, others],
        [pltpu.VMEM((PIECE, VPAD), F32), pltpu.VMEM((KH, VPAD), F32), weight, held, dma(2)],
    )

    gate_query, parcel, base_key_grad, base_value_grad = run(
        back_kernel,
        (
            shape(PIECE, VPAD + HALF),
            shape(PIECE, VPAD + HALF),
            shape(PIECE, HALF, kind=F32),
            shape(PIECE, VPAD, kind=F32),
        ),
        [decay_rate],
        [seg_column, seg_row, queries, keys, values, masked, incoming, grad_retained, grad_gate, gb_oth, mixed],
    )
    parcel_theirs = from_shard(parcel)
    gate_query_theirs = from_shard(gate_query)
    outgoing, _, scanned = exchange(term, True, gate_query)
    mlp_parts, mlp_theirs = hold((mlp_parts, mlp_theirs), scanned)
    mlp_all = all_tokens(mlp_parts, mlp_theirs)
    early_part = outer(
        [
            up_features,
            features_in(core, low2_own, mlp_theirs, 3 * VPAD),
            features_in(core, gb_own, parcel_theirs, VPAD, scanned),
        ],
        [mlp_all, all_tokens(parcel, parcel_theirs)],
        [(0, 0, 0), (1, 0, 1), (1, 0, 2), (2, 1, 0)],
        VPAD,
        4 * VPAD,
    )
    key_value = run(
        later_kernel,
        shape(PIECE, HALF + VPAD),
        [decay_rate],
        [seg_column, seg_row, keys, values, outgoing, base_key_grad, base_value_grad],
        [gate_query_theirs, early_part],
        scratch=[pltpu.VMEM((PIECE, VPAD), F32)],
    )
    key_value_theirs = from_shard(key_value)

    early = lax.psum_scatter(
        after(early_part, outgoing), "ctx", scatter_dimension=0, axis_index_groups=PLANE, tiled=False
    )
    early = early.astype(F32)
    gate_query, gate_query_theirs = hold((gate_query, gate_query_theirs), key_value)
    gate_query_parts = sent(
        outer(
            [low1_features],
            [all_tokens(gate_query, gate_query_theirs)],
            [(0, 0, 0), (0, 0, 1)],
            (VPAD + HALF) // 2,
            VPAD + HALF,
            flops=40 * 10**9,
        )
    )
    first_weights = [query_weight, key_weight, value_turned, gate_turned]
    part, helped = run(
        first_back_kernel,
        (small, small),
        [],
        [gate_query, gate_query_theirs, key_value, key_value_theirs] + first_weights,
    )
    tokens_grad, vec_own, vec_oth = run(
        last_kernel,
        (shape(PIECE, WIDE, kind=F32), shape(16, HALF), shape(16, HALF)),
        [shard],
        [part, from_tp(part), from_shard(helped), lax.ppermute(helped, ("shard", "tp"), SHARD_TP)]
        + [normed1, inverse1, gain1, grad_middle, vectors],
    )
    sums = (
        vec_own,
        from_shard(vec_oth),
        core_swap(vec_own),
        lax.ppermute(vec_oth, ("shard", "ctx"), SHARD_CORE),
    )
    key_value_parts = sent(
        outer(
            [low1_features],
            [all_tokens(key_value, key_value_theirs)],
            [(0, 0, 0), (0, 0, 1)],
            (HALF + VPAD) // 2,
            HALF + VPAD,
            vectors=sums,
            core=core,
            later=(gate_query_parts,),
        )
    )

    part = run(down_kernel, shape(2 * PIECE, HALF), [], [mlp_parts, mlp_theirs, mlp_down])
    down_own, down_gone = run(
        down_sum_kernel, (shape(PIECE, HALF, kind=F32), small), [], [part, from_tp(part)]
    )
    layer_out = run(result_kernel, wide, [shard], [middle, down_own, from_shard(down_gone)])

    gate_query_sums = added(gate_query_parts)
    key_sums, value_sums, norms = run(
        sum_kernel,
        (shape(BLOCK, HALF, kind=F32), shape(BLOCK, VW, kind=F32), shape(BLOCK, 128, kind=F32)),
        [],
        [key_value_parts],
    )
    norms = norms[:, 64:68].T
    early = [early[:, k * VPAD : k * VPAD + VW] for k in range(4)]
    return (
        layer_out[None],
        tokens_grad[None],
        norms[0],
        norms[1],
        gate_query_sums[:, VPAD:],
        key_sums,
        value_sums,
        gate_query_sums[:, :VW],
        early[3].T,
        norms[2],
        norms[3],
        early[1],
        early[2],
        early[0].T,
    )


def solution(mesh):
    in_specs = (
        P("shard", "ctx", None),
        P("shard", "ctx"),
        P("tp"),
        P(),
        P(),
        P("shard", "tp"),
        P("shard", "tp"),
        P("shard", "tp"),
        P("shard", "tp"),
        P("tp", "shard"),
        P(),
        P(),
        P("shard", "tp"),
        P("shard", "tp"),
        P("tp", "shard"),
        P("shard", "ctx", None),
    )
    out_specs = (
        P("shard", "ctx", None),
        P("shard", "ctx", None),
        P(("shard", "ctx")),
        P(("shard", "ctx")),
        P(("shard", "ctx"), "tp"),
        P(("shard", "ctx"), "tp"),
        P(("shard", "ctx"), "tp"),
        P(("shard", "ctx"), "tp"),
        P("tp", ("shard", "ctx")),
        P(("shard", "ctx")),
        P(("shard", "ctx")),
        P(("shard", "ctx"), "tp"),
        P(("shard", "ctx"), "tp"),
        P("tp", ("shard", "ctx")),
    )
    return jax.shard_map(body, mesh=mesh, in_specs=in_specs, out_specs=out_specs, check_vma=False)
```

```python
import functools

import jax
import jax.numpy as jnp
from jax import lax
from jax.experimental import pallas as pl
from jax.experimental.pallas import tpu as pltpu
from jax.sharding import PartitionSpec as P

KH = 256
VH = 432
EPS = 1e-05
BF = jnp.bfloat16
F32 = jnp.float32
F16 = jnp.float16
NC = 32
BLOCK = 32
HALF = 1024
VW = 1728
VPAD = 1792
HEADS = 4
PIECE = 128
QKV = 2 * HALF + VW
GATHERED = 3
PACKED = GATHERED * VPAD
WIDE = 2048

SWAP = [(0, 1), (1, 0)]
CORE = [(index, index ^ 1) for index in range(NC)]
SHARD_TP = [(0, 3), (1, 2), (2, 1), (3, 0)]
SHARD_CORE = [(index, (index ^ 1) ^ NC) for index in range(2 * NC)]
PLANE = [[2 * chip + core for chip in range(16)] for core in range(2)]
ANY = pl.BlockSpec(memory_space=pl.ANY)
SMEM = pl.BlockSpec(memory_space=pltpu.SMEM)


def product(left, right):
    return jnp.dot(left, right, preferred_element_type=F32)


def product_left(left, right):
    return lax.dot_general(left, right, (((0,), (0,)), ((), ())), preferred_element_type=F32)


def product_right(left, right):
    return lax.dot_general(left, right, (((1,), (1,)), ((), ())), preferred_element_type=F32)


def from_shard(part):
    return lax.ppermute(part, "shard", SWAP)


def half_from_shard(part):
    return lax.ppermute(part.astype(F16), "shard", SWAP).astype(F32)


def from_tp(part):
    return lax.ppermute(part, "tp", SWAP)


def core_swap(part):
    return lax.ppermute(part, "ctx", CORE)


def shape(*dims, kind=BF):
    return jax.ShapeDtypeStruct(dims, kind)


def whole(array):
    return pl.BlockSpec(array.shape, lambda i, rank=len(array.shape): (0,) * rank)


def run(kernel, outs, scalars, blocks, far=(), scratch=(), flops=0):
    single = not isinstance(outs, tuple)
    outs = (outs,) if single else outs
    got = pl.pallas_call(
        kernel,
        out_shape=outs,
        grid=(1,),
        in_specs=[SMEM] * len(scalars) + [whole(a) for a in blocks] + [ANY] * len(far),
        out_specs=tuple(whole(a) for a in outs),
        scratch_shapes=list(scratch),
        compiler_params=pltpu.CompilerParams(vmem_limit_bytes=56 * 1024 * 1024),
        cost_estimate=pl.CostEstimate(flops=flops, bytes_accessed=0, transcendentals=0),
    )(*scalars, *blocks, *far)
    return got[0] if single else got


def hold(arrays, *others):
    count = len(arrays)
    return pl.pallas_call(
        lambda *refs: None,
        out_shape=tuple(shape(*a.shape, kind=a.dtype) for a in arrays),
        in_specs=[ANY] * (count + len(others)),
        out_specs=(ANY,) * count,
        input_output_aliases={k: k for k in range(count)},
        cost_estimate=pl.CostEstimate(flops=0, bytes_accessed=0, transcendentals=0),
    )(*arrays, *others)


def after(array, *others):
    return hold((array,), *others)[0]


def fetch(sources, holders, semaphores):
    copies = [pltpu.make_async_copy(src, dst, semaphores.at[k]) for k, (src, dst) in enumerate(zip(sources, holders))]
    for copy in copies:
        copy.start()
    return copies


def part_of(others, k):
    return others.at[:, k * VPAD : (k + 1) * VPAD]


def own_first(shard, array):
    a, b = array[:, :HALF], array[:, HALF:]
    return jnp.where(shard == 0, a, b), jnp.where(shard == 0, b, a)


def normed_of(own, oth):
    mean = (jnp.sum(own, 1, keepdims=True) + jnp.sum(oth, 1, keepdims=True)) / WIDE
    own, oth = own - mean, oth - mean
    var = (jnp.sum(own * own, 1, keepdims=True) + jnp.sum(oth * oth, 1, keepdims=True)) / WIDE
    inverse = lax.rsqrt(var + EPS)
    return own * inverse, oth * inverse, inverse


def norm_back(grads, gains, normed, inverse):
    grads = [grad * gain for grad, gain in zip(grads, gains)]
    mean = sum(jnp.sum(g, 1, keepdims=True) for g in grads) / WIDE
    slant = sum(jnp.sum(g * n, 1, keepdims=True) for g, n in zip(grads, normed)) / WIDE
    return [inverse * (g - mean - n * slant) for g, n in zip(grads, normed)]


def first_kernel(place, shard, tokens, gain, bias, *refs):
    weights, (normed, inverse, low_own, low_oth, packed, columns, semaphores) = refs[:GATHERED], refs[GATHERED:]
    begin = pl.multiple_of(place[0] // 4 * 128, 128)
    copies = fetch([w.at[:, pl.ds(begin, 128)] for w in weights], [columns.at[k] for k in range(GATHERED)], semaphores)
    own, oth = own_first(shard[0], tokens[...].astype(F32))
    own, oth, scale = normed_of(own, oth)
    gains, biases = own_first(shard[0], gain[...]), own_first(shard[0], bias[...])
    normed[:, :HALF] = own
    normed[:, HALF:] = oth
    inverse[...] = jnp.broadcast_to(scale, inverse.shape)
    low_own[...] = (own * gains[0] + biases[0]).astype(BF)
    low_oth[...] = (oth * gains[1] + biases[1]).astype(BF)
    packed[...] = jnp.zeros_like(packed)
    column = lax.broadcasted_iota(jnp.int32, (BLOCK, 128), 1)
    wanted = lax.broadcasted_iota(jnp.int32, (BLOCK, 128), 0) + (place[0] % 4) * BLOCK
    chosen = (column == wanted).astype(F32).astype(BF)
    for k in range(GATHERED):
        copies[k].wait()
        packed[:, k * VPAD : k * VPAD + VW] = product_right(chosen, columns[k]).astype(BF)


def turn_kernel(shard, array, own, oth):
    own[...], oth[...] = own_first(shard[0], array[...])


def help_kernel(low, key_weight, value_weight, key, value):
    key[...] = product(low[...], key_weight[...])
    value[...] = product_right(low[...], value_weight[...])


def help_more_kernel(low, query_weight, gate_weight, query, gate):
    query[...] = product(low[...], query_weight[...])
    gate[...] = product_right(low[...], gate_weight[...])


def base_kernel(low, query_weight, key_weight, value_weight, gate_weight, _, query, key, value, gate):
    query[...] = product(low[...], query_weight[...])
    key[...] = product(low[...], key_weight[...])
    value[...] = product_right(low[...], value_weight[...])
    gate[...] = product_right(low[...], gate_weight[...])


def hidden_kernel(own, theirs, weight, base, helped):
    both = jnp.concatenate([own[...], theirs[...]], 0)
    total = product_right(both, weight[...])
    base[...] = total[:PIECE]
    helped[...] = total[PIECE:]


def window(head):
    begin = head * VH // 128 * 128
    end = -(-(head + 1) * VH // 128) * 128
    return begin, end


def inside(head, rows):
    begin, end = window(head)
    column = lax.broadcasted_iota(jnp.int32, (rows, end - begin), 1) + begin
    return (column >= head * VH) & (column < (head + 1) * VH)


def head_part(ref, head, rows):
    begin, end = window(head)
    return jnp.where(inside(head, rows), ref[:, begin:end].astype(F32), 0.0)


def decay_of(rate, seg_column, seg_row):
    down = lax.broadcasted_iota(jnp.int32, (PIECE, PIECE), 0) - lax.broadcasted_iota(jnp.int32, (PIECE, PIECE), 1)
    near = jnp.exp(-rate * jnp.maximum(down, 0).astype(F32))
    return jnp.where((down >= 0) & (seg_column == seg_row), near, 0.0)


def tail_of(rate, seg_column, seg_row):
    left = (PIECE - 1 - lax.broadcasted_iota(jnp.int32, (PIECE, 1), 0)).astype(F32)
    return jnp.where(seg_column == seg_row[:, PIECE - 1 :], jnp.exp(-rate * left), 0.0)


def reach_of(rate, seg_column, before):
    passed = (lax.broadcasted_iota(jnp.int32, (PIECE, 1), 0) + 1).astype(F32)
    return jnp.where(seg_column == before, jnp.exp(-rate * passed), 0.0)


def with_marks(total, seg_row):
    column = lax.broadcasted_iota(jnp.int32, total.shape, 1)
    marked = jnp.where(column == VW, seg_row[:, :1], jnp.where(column == VW + 1, seg_row[:, PIECE - 1 :], 0.0))
    return jnp.where(column < VW, total, marked).astype(BF)


def mark(states, offset):
    column = lax.broadcasted_iota(jnp.int32, (states.shape[0], 128), 1)
    return jnp.sum(jnp.where(column == VW - (VPAD - 128) + offset, states[:, VPAD - 128 :], 0.0), 1, keepdims=True)


def local_kernel(rates, seg_column, seg_row, base_key, base_value, helped_key, helped_value, _, keys, values, local, total):
    keys[...] = (base_key[...] + helped_key[...].astype(F32)).astype(BF)
    values[:, :VW] = (base_value[...] + helped_value[...].astype(F32)).astype(BF)
    values[:, VW:] = jnp.zeros((PIECE, VPAD - VW), BF)
    total[...] = jnp.zeros_like(total)
    for head in range(HEADS):
        begin, end = window(head)
        own = slice(head * KH, (head + 1) * KH)
        value = head_part(values, head, PIECE).astype(BF)
        key_tail = (keys[:, own].astype(F32) * tail_of(rates[head], seg_column[...], seg_row[...])).astype(BF)
        total[:, begin:end] += product_left(key_tail, value)
    local[...] = with_marks(total[...], seg_row[...])


def inner_kernel(rates, seg_column, seg_row, base_query, helped_query, keys, values, queries, inner, masked):
    queries[...] = (base_query[...] + helped_query[...].astype(F32)).astype(BF)
    inner[...] = jnp.zeros_like(inner)
    for head in range(HEADS):
        begin, end = window(head)
        own = slice(head * KH, (head + 1) * KH)
        scores = product_right(queries[:, own], keys[:, own])
        kept = (scores * decay_of(rates[head], seg_column[...], seg_row[...])).astype(BF)
        masked[head] = kept
        inner[:, begin:end] += product(kept, head_part(values, head, PIECE).astype(BF))


def scan_kernel(reverse, rates, states, *refs):
    out = refs[-1]
    column = lax.broadcasted_iota(jnp.int32, (8, VPAD), 1)
    rate = jnp.full((8, VPAD), rates[HEADS - 1], F32)
    for head in range(HEADS - 1):
        rate = jnp.where((column >= head * VH) & (column < (head + 1) * VH), rates[head], rate)
    factor = jnp.exp(-rate * PIECE)
    edges = [states[p, :, VPAD - 128 :].astype(F32) for p in range(NC)]

    def mark_of(p, offset):
        lane = lax.broadcasted_iota(jnp.int32, (8, 128), 1)
        return jnp.sum(jnp.where(lane == VW - (VPAD - 128) + offset, edges[p], 0.0), 1, keepdims=True)

    firsts = [mark_of(p, 0) for p in range(NC)]
    lasts = [mark_of(p, 1) for p in range(NC)]
    befores = [jnp.full((8, 1), -1.0, F32)] + lasts[:-1]
    carry = jnp.zeros((8, VPAD), F32)
    for k in range(NC):
        p = NC - 1 - k if reverse else k
        out[p] = jnp.where(column < VW, carry, befores[p]).astype(BF)
        keep = jnp.where((firsts[p] == lasts[p]) & (firsts[p] == befores[p]), factor, 0.0)
        carry = states[p].astype(F32) + keep * carry


def mix_kernel(
    rates, seg_column, queries, inner, incoming, base_gate, helped_gate, out_weight, others, _,
    gate, grouped, inverse, mixed, part, total, held, near, semaphores,
):
    copies = fetch([out_weight, part_of(others, 2)], [near, held], semaphores)
    gate[...] = base_gate[...] + helped_gate[...].astype(F32)
    before = mark(incoming[:16].astype(F32), 0)[:1]
    total[...] = inner[...]
    for head in range(HEADS):
        begin, end = window(head)
        own = slice(head * KH, (head + 1) * KH)
        across = product(queries[:, own], incoming[:, begin:end])
        total[:, begin:end] += jnp.where(
            inside(head, PIECE), reach_of(rates[head], seg_column[...], before) * across, 0.0
        )
    lane = lax.broadcasted_iota(jnp.int32, (PIECE, 128), 1)
    scales = jnp.zeros((PIECE, 128), F32)
    grouped[...] = jnp.zeros_like(grouped)
    for head in range(HEADS):
        begin, end = window(head)
        here = inside(head, PIECE)
        retained = jnp.where(here, total[:, begin:end], 0.0)
        center = jnp.where(here, retained - jnp.sum(retained, 1, keepdims=True) / VH, 0.0)
        scale = lax.rsqrt(jnp.sum(center * center, 1, keepdims=True) / VH + EPS)
        grouped[:, begin:end] += center * scale
        scales = jnp.where(lane == head, scale, scales)
    inverse[...] = scales
    mixed[:, :VW] = (jax.nn.silu(gate[...]) * grouped[:, :VW]).astype(BF)
    mixed[:, VW:] = jnp.zeros((PIECE, VPAD - VW), BF)
    copies[0].wait()
    part[:, :HALF] = product(mixed[:, :VW], near[...]).astype(BF)
    copies[1].wait()
    part[:, HALF:] = product_right(mixed[...], held[...]).astype(BF)


def mlp_kernel(
    shard, tokens, mine, theirs, gain, bias, base_hidden, helped_hidden, gate_weight, up_weight, others, _up, _low,
    middle, normed, inverse, low_own, grads, part,
    near_gate, near_up, far_gate, far_up, semaphores,
):
    copies = fetch(
        [gate_weight, part_of(others, 0), up_weight, part_of(others, 1)],
        [near_gate, far_gate, near_up, far_up],
        semaphores,
    )
    own, oth = own_first(shard[0], tokens[...].astype(F32))
    own = own + (mine[:, :HALF].astype(F32) + theirs[:, :HALF].astype(F32))
    oth = oth + (mine[:, HALF:].astype(F32) + theirs[:, HALF:].astype(F32))
    middle[:, :HALF] = own
    middle[:, HALF:] = oth
    own, oth, scale = normed_of(own, oth)
    gains, biases = own_first(shard[0], gain[...]), own_first(shard[0], bias[...])
    normed[:, :HALF] = own
    normed[:, HALF:] = oth
    inverse[...] = jnp.broadcast_to(scale, inverse.shape)
    low_own[...] = (own * gains[0] + biases[0]).astype(BF)
    low_oth = (oth * gains[1] + biases[1]).astype(BF)
    grads[:, 3 * VPAD :] = low_oth
    copies[0].wait()
    up_gate = product_right(low_own[...], near_gate[...])
    copies[1].wait()
    up_gate += product(low_oth, far_gate[:, :VW])
    copies[2].wait()
    up_vals = product_right(low_own[...], near_up[...])
    copies[3].wait()
    up_vals += product(low_oth, far_up[:, :VW])
    grad_hidden = base_hidden[...] + helped_hidden[...].astype(F32)
    sigma = jax.nn.sigmoid(up_gate)
    silu = up_gate * sigma
    none = jnp.zeros((PIECE, VPAD - VW), BF)
    for k, array in enumerate(
        (silu * up_vals, grad_hidden * up_vals * (sigma * (1.0 + up_gate * (1.0 - sigma))), grad_hidden * silu)
    ):
        grads[:, k * VPAD : k * VPAD + VW] = array.astype(BF)
        grads[:, k * VPAD + VW : (k + 1) * VPAD] = none
    total = product(grads[:, VPAD : VPAD + VW], near_gate[...])
    total += product(grads[:, 2 * VPAD : 2 * VPAD + VW], near_up[...])
    part[:, :HALF] = total.astype(BF)
    total = product_right(grads[:, VPAD : 2 * VPAD], far_gate[...])
    total += product_right(grads[:, 2 * VPAD : 3 * VPAD], far_up[...])
    part[:, HALF:] = total.astype(BF)


def down_kernel(own, theirs, weight, part):
    both = jnp.concatenate([own[:, :VW], theirs[:, :VW]], 0)
    part[...] = product(both, weight[...]).astype(BF)


def down_sum_kernel(mine, theirs, own, gone):
    own[...] = mine[:PIECE].astype(F32) + theirs[:PIECE].astype(F32)
    gone[...] = (mine[PIECE:].astype(F32) + theirs[PIECE:].astype(F32)).astype(BF)


def result_kernel(shard, middle, own, oth, out):
    total = [middle[:, :HALF] + own[...], middle[:, HALF:] + oth[...].astype(F32)]
    out[:, :HALF] = jnp.where(shard[0] == 0, total[0], total[1]).astype(BF)
    out[:, HALF:] = jnp.where(shard[0] == 0, total[1], total[0]).astype(BF)


def unmix_kernel(
    shard, rates, mine, theirs, normed, inverse, gain, up_own, up_oth, seg_column, seg_row, queries, incoming, gate,
    grouped, scales, out_weight, others,
    grad_middle, branch_own, branch_oth, vectors, grad_gate, grad_retained, term,
    held, total, near, far, semaphores,
):
    copies = fetch([out_weight, part_of(others, 2)], [near, far], semaphores)
    grads = [mine[:, cut].astype(F32) + theirs[:, cut].astype(F32) for cut in (slice(0, HALF), slice(HALF, WIDE))]
    norms = [normed[:, :HALF], normed[:, HALF:]]
    vectors[...] = jnp.zeros_like(vectors)
    for k in range(2):
        cut = slice(k * HALF, (k + 1) * HALF)
        vectors[0:1, cut] = jnp.sum(grads[k] * norms[k], 0, keepdims=True)
        vectors[1:2, cut] = jnp.sum(grads[k], 0, keepdims=True)
    back = norm_back(grads, own_first(shard[0], gain[...]), norms, inverse[:, :1])
    own, oth = up_own[...].astype(F32) + back[0], up_oth[...].astype(F32) + back[1]
    grad_middle[:, :HALF] = own
    grad_middle[:, HALF:] = oth
    branch_own[...] = own.astype(BF)
    branch_oth[...] = oth.astype(BF)
    before = mark(incoming[:16].astype(F32), 0)[:1]
    sigma = jax.nn.sigmoid(gate[...])
    copies[0].wait()
    grad_mixed = product_right(branch_own[...], near[...])
    copies[1].wait()
    grad_mixed += product(branch_oth[...], far[:, :VW])
    slope = sigma * (1.0 + gate[...] * (1.0 - sigma))
    none = jnp.zeros((PIECE, VPAD - VW), F32)
    grad_gate[:, :VW] = (grad_mixed * grouped[:, :VW] * slope).astype(BF)
    grad_gate[:, VW:] = none.astype(BF)
    held[:, :VW] = grad_mixed * (gate[...] * sigma)
    held[:, VW:] = none
    lane = lax.broadcasted_iota(jnp.int32, (PIECE, 128), 1)
    total[...] = jnp.zeros_like(total)
    for head in range(HEADS):
        begin, end = window(head)
        here = inside(head, PIECE)
        grad = head_part(held, head, PIECE)
        group = head_part(grouped, head, PIECE)
        scale = jnp.sum(jnp.where(lane == head, scales[...], 0.0), 1, keepdims=True)
        back = grad - jnp.sum(grad, 1, keepdims=True) / VH - group * (jnp.sum(grad * group, 1, keepdims=True) / VH)
        total[:PIECE, begin:end] += jnp.where(here, scale * back, 0.0)
    grad_retained[...] = total[:PIECE].astype(BF)
    total[...] = jnp.zeros_like(total)
    for head in range(HEADS):
        begin, end = window(head)
        own = slice(head * KH, (head + 1) * KH)
        reached = reach_of(rates[head], seg_column[...], before) * head_part(grad_retained, head, PIECE)
        total[:, begin:end] += product_left(queries[:, own], reached.astype(BF))
    term[...] = with_marks(total[...], seg_row[...])


def back_kernel(
    rates, seg_column, seg_row, queries, keys, values, masked, incoming, grad_retained, grad_gate, gb, mixed,
    gate_query, parcel, base_key, base_value,
):
    before = mark(incoming[:16].astype(F32), 0)[:1]
    gate_query[:, :VPAD] = grad_gate[...]
    base_value[...] = jnp.zeros_like(base_value)
    for head in range(HEADS):
        rate = rates[head]
        begin, end = window(head)
        own = slice(head * KH, (head + 1) * KH)
        value = head_part(values, head, PIECE).astype(BF)
        grad = head_part(grad_retained, head, PIECE).astype(BF)
        decay = decay_of(rate, seg_column[...], seg_row[...])
        reach = reach_of(rate, seg_column[...], before)
        grad_scores = (product_right(grad, value) * decay).astype(BF)
        grad_query = product(grad_scores, keys[:, own])
        grad_query += reach * product_right(grad, incoming[:, begin:end])
        gate_query[:, VPAD + head * KH : VPAD + (head + 1) * KH] = grad_query.astype(BF)
        base_key[:, own] = product_left(grad_scores, queries[:, own])
        base_value[:, begin:end] += product_left(masked[head], grad)
    parcel[:, :VPAD] = mixed[...]
    parcel[:, VPAD:] = gb[...]


def later_kernel(rates, seg_column, seg_row, keys, values, outgoing, base_key, base_value, _theirs, _early, out, total):
    total[...] = base_value[...]
    for head in range(HEADS):
        begin, end = window(head)
        own = slice(head * KH, (head + 1) * KH)
        value = head_part(values, head, PIECE).astype(BF)
        tail = tail_of(rates[head], seg_column[...], seg_row[...])
        grad_key = base_key[:, own] + tail * product_right(value, outgoing[:, begin:end])
        out[:, own] = grad_key.astype(BF)
        total[:, begin:end] += jnp.where(inside(head, PIECE), tail * product(keys[:, own], outgoing[:, begin:end]), 0.0)
    out[:, HALF:] = total[...].astype(BF)


def first_back_kernel(
    gate_query, gate_query_theirs, key_value, key_value_theirs, query_weight, key_weight, value_weight, gate_weight,
    part, helped,
):
    both = jnp.concatenate([gate_query[...], gate_query_theirs[...]], 0)
    total = product_right(both[:, VPAD : VPAD + HALF], query_weight[...])
    total += product(both[:, :VW], gate_weight[...])
    both = jnp.concatenate([key_value[...], key_value_theirs[...]], 0)
    total += product_right(both[:, :HALF], key_weight[...])
    total += product(both[:, HALF : HALF + VW], value_weight[...])
    part[...] = total[:PIECE].astype(BF)
    helped[...] = total[PIECE:].astype(BF)


def last_kernel(
    shard, mine, theirs, helped, helped_other, normed, inverse, gain, grad_middle, vectors, out, vec_own, vec_oth
):
    grads = [
        mine[...].astype(F32) + theirs[...].astype(F32),
        helped[...].astype(F32) + helped_other[...].astype(F32),
    ]
    norms = [normed[:, :HALF], normed[:, HALF:]]
    for k, vec in enumerate((vec_own, vec_oth)):
        cut = slice(k * HALF, (k + 1) * HALF)
        rows = [jnp.sum(grads[k] * norms[k], 0, keepdims=True), jnp.sum(grads[k], 0, keepdims=True)]
        rows += [vectors[0:1, cut], vectors[1:2, cut], jnp.zeros((12, HALF), F32)]
        vec[...] = jnp.concatenate(rows, 0).astype(BF)
    back = norm_back(grads, own_first(shard[0], gain[...]), norms, inverse[:, :1])
    total = [grad_middle[:, :HALF] + back[0], grad_middle[:, HALF:] + back[1]]
    out[:, :HALF] = jnp.where(shard[0] == 0, total[0], total[1])
    out[:, HALF:] = jnp.where(shard[0] == 0, total[1], total[0])


def rows_of(core):
    column = lax.broadcasted_iota(jnp.int32, (HALF // 2, HALF), 1)
    row = lax.broadcasted_iota(jnp.int32, (HALF // 2, HALF), 0)
    source = (row // BLOCK * 2 + core) * BLOCK + row % BLOCK
    return (column == source).astype(F32).astype(BF)


def rows_kernel(core, *refs):
    count = (len(refs) - 2) // 2
    for chosen, out in ((core[0], refs[-2]), (1 - core[0], refs[-1])):
        pick = rows_of(chosen)
        for k in range(2 * count):
            out[:, k * PIECE : (k + 1) * PIECE] = product_right(pick, refs[k][...]).astype(BF)


def rows_cut_kernel(start, core, own, sent, *refs):
    kept, gone = refs[-2:]
    for chosen, out in ((core[0], kept), (1 - core[0], gone)):
        pick = rows_of(chosen)
        out[:, :PIECE] = product_right(pick, own[...]).astype(BF)
        out[:, PIECE:] = product_right(pick, sent[:, start : start + HALF]).astype(BF)


def features_of(core, own, received):
    both = shape(HALF // 2, 2 * PIECE)
    kept, gone = run(rows_kernel, (both, both), [core], [own, received])
    return kept, core_swap(gone)


def features_in(core, own, sent, start, *later):
    both = shape(HALF // 2, 2 * PIECE)
    kept, gone = run(functools.partial(rows_cut_kernel, start), (both, both), [core], [own, sent], later)
    return kept, core_swap(gone)


def all_tokens(array, other):
    return (array, other, core_swap(array), core_swap(other))


def outer(features, groups, plan, chunk, width, vectors=None, core=None, later=(), flops=0):
    steps = len(plan)
    flat = [a for pair in features for a in pair]
    flat += [a for group in groups for a in group] + list(vectors or ())
    specs = [pl.BlockSpec((HALF // 2, 2 * PIECE), lambda i, c: (0, 0))] * (2 * len(features))
    for g in range(len(groups)):
        mine = [k for k in range(steps) if plan[k][1] == g]
        first, count, block = mine[0], len(mine), plan[mine[0]][2]
        assert mine == list(range(first, first + count))

        def place(i, c, first=first, count=count, block=block):
            return (0, block + jnp.clip(i - first, 0, count - 1))

        specs += [pl.BlockSpec((PIECE, chunk), place)] * 4
    specs += [pl.BlockSpec((16, HALF), lambda i, c: (0, 0))] * len(vectors or ())
    specs += [ANY] * len(later)
    flat += list(later)

    def chosen(step, column, choices):
        value = choices[plan[0][column]]
        for k in range(1, steps):
            if plan[k][column] != plan[k - 1][column]:
                value = jnp.where(step >= k, choices[plan[k][column]], value)
        return value

    def kernel(core, *refs):
        out = refs[-1]
        step = pl.program_id(0)
        count = 2 * len(features)
        left = [
            jnp.concatenate([refs[2 * k][...], refs[2 * k + 1][...]], 1) for k in range(len(features))
        ]
        right = [
            jnp.concatenate([refs[count + 4 * k + j][...] for j in range(4)], 0) for k in range(len(groups))
        ]
        out[...] = product(chosen(step, 0, left), chosen(step, 1, right)).astype(BF)
        if vectors is not None:

            @pl.when(step == steps - 1)
            def _():
                rows = refs[count + 4 * len(groups) :]
                total = (rows[0][...].astype(F32) + rows[1][...].astype(F32)) + (
                    rows[2][...].astype(F32) + rows[3][...].astype(F32)
                )
                column = lax.broadcasted_iota(jnp.int32, (16, 128), 1)
                row = lax.broadcasted_iota(jnp.int32, (16, 128), 0)
                shift = (column == row + 64).astype(F32).astype(BF)
                moved = product(product_right(rows_of(core[0]), total.astype(BF)).astype(BF), shift)
                out[:, chunk - 128 :] = (out[:, chunk - 128 :].astype(F32) + moved).astype(BF)

    if core is None:
        core = jnp.zeros((1,), jnp.int32)
    part = pl.pallas_call(
        kernel,
        out_shape=shape(HALF // 2, width),
        grid_spec=pltpu.PrefetchScalarGridSpec(
            num_scalar_prefetch=1,
            grid=(steps,),
            in_specs=specs,
            out_specs=pl.BlockSpec((HALF // 2, chunk), lambda i, c: (0, i)),
        ),
        compiler_params=pltpu.CompilerParams(vmem_limit_bytes=56 * 1024 * 1024),
        cost_estimate=pl.CostEstimate(flops=flops, bytes_accessed=0, transcendentals=0),
    )(core, *flat)
    return part.reshape(16, BLOCK, width)


def sum_kernel(parts, key, value, norms):
    total = parts[0].astype(F32)
    for k in range(1, 16):
        total += parts[k].astype(F32)
    key[...] = total[:, :HALF]
    value[...] = total[:, HALF : HALF + VW]
    norms[...] = total[:, HALF + VPAD - 128 :]


def sent(part):
    return lax.all_to_all(part, "ctx", 0, 0, axis_index_groups=PLANE, tiled=True)


def added(parts):
    return jnp.sum(parts.astype(F32), 0)


def body(
    tokens,
    segments,
    decay_rate,
    first_gain,
    first_bias,
    query_weight,
    key_weight,
    value_weight,
    gate_weight,
    out_weight,
    second_gain,
    second_bias,
    mlp_gate,
    mlp_up,
    mlp_down,
    upstream,
):
    shard = lax.axis_index("shard").astype(jnp.int32).reshape(1)
    ctx = lax.axis_index("ctx").astype(jnp.int32).reshape(1)
    core = ctx % 2
    tokens, upstream = tokens[0], upstream[0]
    value_turned, gate_turned, mlp_gate_turned, mlp_up_turned = value_weight.T, gate_weight.T, mlp_gate.T, mlp_up.T
    gain1, bias1, gain2, bias2 = first_gain[None], first_bias[None], second_gain[None], second_bias[None]
    seg = segments[0].astype(F32)
    seg_column, seg_row = seg[:, None], seg[None, :]
    weight = pltpu.VMEM((VW, HALF), BF)
    held = pltpu.VMEM((HALF, VPAD), BF)
    small = shape(PIECE, HALF)
    wide = shape(PIECE, WIDE)
    scale = shape(PIECE, 128, kind=F32)

    def dma(count):
        return pltpu.SemaphoreType.DMA((count,))

    normed1, inverse1, low1_own, low1_oth, packed = run(
        first_kernel,
        (shape(PIECE, WIDE, kind=F32), scale, small, small, shape(BLOCK, PACKED)),
        [ctx, shard],
        [tokens, gain1, bias1],
        [mlp_gate_turned, mlp_up_turned, out_weight],
        [pltpu.VMEM((GATHERED, VW, 128), BF), dma(GATHERED)],
    )
    low1_theirs = from_shard(low1_oth)
    packed = from_shard(after(packed, low1_theirs))
    theirs_key, theirs_value = run(
        help_kernel,
        (shape(PIECE, HALF, kind=F32), shape(PIECE, VW, kind=F32)),
        [],
        [low1_theirs, key_weight, value_turned],
    )
    helped_key, helped_value = from_shard(theirs_key), half_from_shard(theirs_value)
    theirs_query, theirs_gate = run(
        help_more_kernel,
        (shape(PIECE, HALF, kind=F32), shape(PIECE, VW, kind=F32)),
        [],
        [low1_theirs, query_weight, gate_turned],
    )
    helped_query, helped_gate = from_shard(theirs_query), half_from_shard(theirs_gate)
    base_query, base_key, base_value, base_gate = run(
        base_kernel,
        tuple(shape(PIECE, n, kind=F32) for n in (HALF, HALF, VW, VW)),
        [],
        [low1_own, query_weight, key_weight, value_turned, gate_turned],
        [theirs_key],
    )

    up_own, up_oth = run(turn_kernel, (small, small), [shard], [upstream])
    up_theirs = from_shard(up_oth)
    others = lax.all_gather(after(packed, theirs_value, up_theirs), "ctx", axis=0, tiled=True)


    def exchange(states, reverse, *before):
        mine = lax.all_to_all(states.reshape(NC, KH // NC, VPAD), "ctx", 0, 0, tiled=True)
        done = run(functools.partial(scan_kernel, reverse), shape(NC, KH // NC, VPAD), [decay_rate], [mine], before)
        return lax.all_to_all(done, "ctx", 0, 0, tiled=True).reshape(KH, VPAD), mine, done

    keys, values, local = run(
        local_kernel,
        (small, shape(PIECE, VPAD), shape(KH, VPAD)),
        [decay_rate],
        [seg_column, seg_row, base_key, base_value, helped_key, helped_value],
        [theirs_query],
        scratch=[pltpu.VMEM((KH, VPAD), F32)],
    )
    base_hidden, theirs_hidden = run(
        hidden_kernel,
        (shape(PIECE, VW, kind=F32), shape(PIECE, VW, kind=F32)),
        [],
        [up_own, up_theirs, mlp_down],
    )
    helped_hidden = half_from_shard(theirs_hidden)
    incoming, _, _ = exchange(local, False, helped_query, helped_gate, theirs_hidden)
    queries, inner, masked = run(
        inner_kernel,
        (small, shape(PIECE, VPAD, kind=F32), shape(HEADS, PIECE, PIECE)),
        [decay_rate],
        [seg_column, seg_row, base_query, helped_query, keys, values],
    )
    up_features = features_of(core, up_own, up_theirs)
    low1_features = features_of(core, low1_own, low1_theirs)
    gate_pre, grouped, scales, mixed, part = run(
        mix_kernel,
        (shape(PIECE, VW, kind=F32), shape(PIECE, VPAD, kind=F32), scale, shape(PIECE, VPAD), wide),
        [decay_rate],
        [seg_column, queries, inner, incoming, base_gate, helped_gate],
        [out_weight, others, helped_hidden],
        [pltpu.VMEM((PIECE, VPAD), F32), held, weight, dma(2)],
    )
    theirs = from_tp(part)
    middle, normed2, inverse2, low2_own, mlp_parts, part = run(
        mlp_kernel,
        (shape(PIECE, WIDE, kind=F32), shape(PIECE, WIDE, kind=F32), scale, small, shape(PIECE, 3 * VPAD + HALF), wide),
        [shard],
        [tokens, part, theirs, gain2, bias2, base_hidden, helped_hidden],
        [mlp_gate_turned, mlp_up_turned, others, up_features[1], low1_features[1]],
        [weight, weight, held, held, dma(4)],
    )
    theirs = from_tp(part)
    mlp_parts = after(mlp_parts, theirs)
    mlp_theirs = from_shard(mlp_parts)
    grad_middle, gb_own, gb_oth, vectors, grad_gate, grad_retained, term = run(
        unmix_kernel,
        (
            shape(PIECE, WIDE, kind=F32),
            small,
            small,
            shape(8, WIDE, kind=F32),
            shape(PIECE, VPAD),
            shape(PIECE, VPAD),
            shape(KH, VPAD),
        ),
        [shard, decay_rate],
        [part, theirs, normed2, inverse2, gain2, up_own, up_oth]
        + [seg_column, seg_row, queries, incoming, gate_pre, grouped, scales],
        [out_weight, others],
        [pltpu.VMEM((PIECE, VPAD), F32), pltpu.VMEM((KH, VPAD), F32), weight, held, dma(2)],
    )

    gate_query, parcel, base_key_grad, base_value_grad = run(
        back_kernel,
        (
            shape(PIECE, VPAD + HALF),
            shape(PIECE, VPAD + HALF),
            shape(PIECE, HALF, kind=F32),
            shape(PIECE, VPAD, kind=F32),
        ),
        [decay_rate],
        [seg_column, seg_row, queries, keys, values, masked, incoming, grad_retained, grad_gate, gb_oth, mixed],
    )
    parcel_theirs = from_shard(parcel)
    gate_query_theirs = from_shard(gate_query)
    outgoing, _, scanned = exchange(term, True, gate_query)
    mlp_parts, mlp_theirs = hold((mlp_parts, mlp_theirs), scanned)
    mlp_all = all_tokens(mlp_parts, mlp_theirs)
    early_part = outer(
        [
            up_features,
            features_in(core, low2_own, mlp_theirs, 3 * VPAD),
            features_in(core, gb_own, parcel_theirs, VPAD, scanned),
        ],
        [mlp_all, all_tokens(parcel, parcel_theirs)],
        [(0, 0, 0), (1, 0, 1), (1, 0, 2), (2, 1, 0)],
        VPAD,
        4 * VPAD,
    )
    early_part = after(early_part, outgoing)
    key_value = run(
        later_kernel,
        shape(PIECE, HALF + VPAD),
        [decay_rate],
        [seg_column, seg_row, keys, values, outgoing, base_key_grad, base_value_grad],
        [gate_query_theirs, early_part],
        scratch=[pltpu.VMEM((PIECE, VPAD), F32)],
    )
    key_value_theirs = from_shard(key_value)

    early = lax.psum_scatter(early_part, "ctx", scatter_dimension=0, axis_index_groups=PLANE, tiled=False)
    early = early.astype(F32)
    gate_query, gate_query_theirs = hold((gate_query, gate_query_theirs), key_value)
    gate_query_parts = sent(
        outer(
            [low1_features],
            [all_tokens(gate_query, gate_query_theirs)],
            [(0, 0, 0), (0, 0, 1)],
            (VPAD + HALF) // 2,
            VPAD + HALF,
            flops=100 * 10**9,
        )
    )
    first_weights = [query_weight, key_weight, value_turned, gate_turned]
    part, helped = run(
        first_back_kernel,
        (small, small),
        [],
        [gate_query, gate_query_theirs, key_value, key_value_theirs] + first_weights,
    )
    tokens_grad, vec_own, vec_oth = run(
        last_kernel,
        (shape(PIECE, WIDE, kind=F32), shape(16, HALF), shape(16, HALF)),
        [shard],
        [part, from_tp(part), from_shard(helped), lax.ppermute(helped, ("shard", "tp"), SHARD_TP)]
        + [normed1, inverse1, gain1, grad_middle, vectors],
    )
    sums = (
        vec_own,
        from_shard(vec_oth),
        core_swap(vec_own),
        lax.ppermute(vec_oth, ("shard", "ctx"), SHARD_CORE),
    )
    key_value_parts = sent(
        outer(
            [low1_features],
            [all_tokens(key_value, key_value_theirs)],
            [(0, 0, 0), (0, 0, 1)],
            (HALF + VPAD) // 2,
            HALF + VPAD,
            vectors=sums,
            core=core,
            later=(gate_query_parts,),
        )
    )

    part = run(down_kernel, shape(2 * PIECE, HALF), [], [mlp_parts, mlp_theirs, mlp_down])
    down_own, down_gone = run(
        down_sum_kernel, (shape(PIECE, HALF, kind=F32), small), [], [part, from_tp(part)]
    )
    layer_out = run(result_kernel, wide, [shard], [middle, down_own, from_shard(down_gone)])

    gate_query_sums = added(gate_query_parts)
    key_sums, value_sums, norms = run(
        sum_kernel,
        (shape(BLOCK, HALF, kind=F32), shape(BLOCK, VW, kind=F32), shape(BLOCK, 128, kind=F32)),
        [],
        [key_value_parts],
    )
    norms = norms[:, 64:68].T
    early = [early[:, k * VPAD : k * VPAD + VW] for k in range(4)]
    return (
        layer_out[None],
        tokens_grad[None],
        norms[0],
        norms[1],
        gate_query_sums[:, VPAD:],
        key_sums,
        value_sums,
        gate_query_sums[:, :VW],
        early[3].T,
        norms[2],
        norms[3],
        early[1],
        early[2],
        early[0].T,
    )


def solution(mesh):
    in_specs = (
        P("shard", "ctx", None),
        P("shard", "ctx"),
        P("tp"),
        P(),
        P(),
        P("shard", "tp"),
        P("shard", "tp"),
        P("shard", "tp"),
        P("shard", "tp"),
        P("tp", "shard"),
        P(),
        P(),
        P("shard", "tp"),
        P("shard", "tp"),
        P("tp", "shard"),
        P("shard", "ctx", None),
    )
    out_specs = (
        P("shard", "ctx", None),
        P("shard", "ctx", None),
        P(("shard", "ctx")),
        P(("shard", "ctx")),
        P(("shard", "ctx"), "tp"),
        P(("shard", "ctx"), "tp"),
        P(("shard", "ctx"), "tp"),
        P(("shard", "ctx"), "tp"),
        P("tp", ("shard", "ctx")),
        P(("shard", "ctx")),
        P(("shard", "ctx")),
        P(("shard", "ctx"), "tp"),
        P(("shard", "ctx"), "tp"),
        P("tp", ("shard", "ctx")),
    )
    return jax.shard_map(body, mesh=mesh, in_specs=in_specs, out_specs=out_specs, check_vma=False)
```

```python
import functools

import jax
import jax.numpy as jnp
from jax import lax
from jax.experimental import pallas as pl
from jax.experimental.pallas import tpu as pltpu
from jax.sharding import PartitionSpec as P

KH = 256
VH = 432
EPS = 1e-05
BF = jnp.bfloat16
F32 = jnp.float32
F16 = jnp.float16
NC = 32
BLOCK = 32
HALF = 1024
VW = 1728
VPAD = 1792
HEADS = 4
PIECE = 128
QKV = 2 * HALF + VW
GATHERED = 3
PACKED = GATHERED * VPAD
WIDE = 2048

SWAP = [(0, 1), (1, 0)]
CORE = [(index, index ^ 1) for index in range(NC)]
SHARD_TP = [(0, 3), (1, 2), (2, 1), (3, 0)]
SHARD_CORE = [(index, (index ^ 1) ^ NC) for index in range(2 * NC)]
PLANE = [[2 * chip + core for chip in range(16)] for core in range(2)]
ANY = pl.BlockSpec(memory_space=pl.ANY)
SMEM = pl.BlockSpec(memory_space=pltpu.SMEM)


def product(left, right):
    return jnp.dot(left, right, preferred_element_type=F32)


def product_left(left, right):
    return lax.dot_general(left, right, (((0,), (0,)), ((), ())), preferred_element_type=F32)


def product_right(left, right):
    return lax.dot_general(left, right, (((1,), (1,)), ((), ())), preferred_element_type=F32)


def from_shard(part):
    return lax.ppermute(part, "shard", SWAP)


def half_from_shard(part):
    return lax.ppermute(part.astype(F16), "shard", SWAP).astype(F32)


def from_tp(part):
    return lax.ppermute(part, "tp", SWAP)


def core_swap(part):
    return lax.ppermute(part, "ctx", CORE)


def shape(*dims, kind=BF):
    return jax.ShapeDtypeStruct(dims, kind)


def whole(array):
    return pl.BlockSpec(array.shape, lambda i, rank=len(array.shape): (0,) * rank)


def run(kernel, outs, scalars, blocks, far=(), scratch=(), flops=0):
    single = not isinstance(outs, tuple)
    outs = (outs,) if single else outs
    got = pl.pallas_call(
        kernel,
        out_shape=outs,
        grid=(1,),
        in_specs=[SMEM] * len(scalars) + [whole(a) for a in blocks] + [ANY] * len(far),
        out_specs=tuple(whole(a) for a in outs),
        scratch_shapes=list(scratch),
        compiler_params=pltpu.CompilerParams(vmem_limit_bytes=56 * 1024 * 1024),
        cost_estimate=pl.CostEstimate(flops=flops, bytes_accessed=0, transcendentals=0),
    )(*scalars, *blocks, *far)
    return got[0] if single else got


def hold(arrays, *others):
    count = len(arrays)
    return pl.pallas_call(
        lambda *refs: None,
        out_shape=tuple(shape(*a.shape, kind=a.dtype) for a in arrays),
        in_specs=[ANY] * (count + len(others)),
        out_specs=(ANY,) * count,
        input_output_aliases={k: k for k in range(count)},
        cost_estimate=pl.CostEstimate(flops=0, bytes_accessed=0, transcendentals=0),
    )(*arrays, *others)


def after(array, *others):
    return hold((array,), *others)[0]


def fetch(sources, holders, semaphores):
    copies = [pltpu.make_async_copy(src, dst, semaphores.at[k]) for k, (src, dst) in enumerate(zip(sources, holders))]
    for copy in copies:
        copy.start()
    return copies


def part_of(others, k):
    return others.at[:, k * VPAD : (k + 1) * VPAD]


def own_first(shard, array):
    a, b = array[:, :HALF], array[:, HALF:]
    return jnp.where(shard == 0, a, b), jnp.where(shard == 0, b, a)


def normed_of(own, oth):
    mean = (jnp.sum(own, 1, keepdims=True) + jnp.sum(oth, 1, keepdims=True)) / WIDE
    own, oth = own - mean, oth - mean
    var = (jnp.sum(own * own, 1, keepdims=True) + jnp.sum(oth * oth, 1, keepdims=True)) / WIDE
    inverse = lax.rsqrt(var + EPS)
    return own * inverse, oth * inverse, inverse


def norm_back(grads, gains, normed, inverse):
    grads = [grad * gain for grad, gain in zip(grads, gains)]
    mean = sum(jnp.sum(g, 1, keepdims=True) for g in grads) / WIDE
    slant = sum(jnp.sum(g * n, 1, keepdims=True) for g, n in zip(grads, normed)) / WIDE
    return [inverse * (g - mean - n * slant) for g, n in zip(grads, normed)]


def first_kernel(place, shard, tokens, gain, bias, *refs):
    weights, (normed, inverse, low_own, low_oth, packed, columns, semaphores) = refs[:GATHERED], refs[GATHERED:]
    begin = pl.multiple_of(place[0] // 4 * 128, 128)
    copies = fetch([w.at[:, pl.ds(begin, 128)] for w in weights], [columns.at[k] for k in range(GATHERED)], semaphores)
    own, oth = own_first(shard[0], tokens[...].astype(F32))
    own, oth, scale = normed_of(own, oth)
    gains, biases = own_first(shard[0], gain[...]), own_first(shard[0], bias[...])
    normed[:, :HALF] = own
    normed[:, HALF:] = oth
    inverse[...] = jnp.broadcast_to(scale, inverse.shape)
    low_own[...] = (own * gains[0] + biases[0]).astype(BF)
    low_oth[...] = (oth * gains[1] + biases[1]).astype(BF)
    packed[...] = jnp.zeros_like(packed)
    column = lax.broadcasted_iota(jnp.int32, (BLOCK, 128), 1)
    wanted = lax.broadcasted_iota(jnp.int32, (BLOCK, 128), 0) + (place[0] % 4) * BLOCK
    chosen = (column == wanted).astype(F32).astype(BF)
    for k in range(GATHERED):
        copies[k].wait()
        packed[:, k * VPAD : k * VPAD + VW] = product_right(chosen, columns[k]).astype(BF)


def turn_kernel(shard, array, own, oth):
    own[...], oth[...] = own_first(shard[0], array[...])


def help_kernel(low, key_weight, value_weight, key, value):
    key[...] = product(low[...], key_weight[...])
    value[...] = product_right(low[...], value_weight[...])


def help_more_kernel(low, query_weight, gate_weight, query, gate):
    query[...] = product(low[...], query_weight[...])
    gate[...] = product_right(low[...], gate_weight[...])


def base_kernel(low, query_weight, key_weight, value_weight, gate_weight, _, query, key, value, gate):
    query[...] = product(low[...], query_weight[...])
    key[...] = product(low[...], key_weight[...])
    value[...] = product_right(low[...], value_weight[...])
    gate[...] = product_right(low[...], gate_weight[...])


def hidden_kernel(own, theirs, weight, base, helped):
    both = jnp.concatenate([own[...], theirs[...]], 0)
    total = product_right(both, weight[...])
    base[...] = total[:PIECE]
    helped[...] = total[PIECE:]


def window(head):
    begin = head * VH // 128 * 128
    end = -(-(head + 1) * VH // 128) * 128
    return begin, end


def inside(head, rows):
    begin, end = window(head)
    column = lax.broadcasted_iota(jnp.int32, (rows, end - begin), 1) + begin
    return (column >= head * VH) & (column < (head + 1) * VH)


def head_part(ref, head, rows):
    begin, end = window(head)
    return jnp.where(inside(head, rows), ref[:, begin:end].astype(F32), 0.0)


def decay_of(rate, seg_column, seg_row):
    down = lax.broadcasted_iota(jnp.int32, (PIECE, PIECE), 0) - lax.broadcasted_iota(jnp.int32, (PIECE, PIECE), 1)
    near = jnp.exp(-rate * jnp.maximum(down, 0).astype(F32))
    return jnp.where((down >= 0) & (seg_column == seg_row), near, 0.0)


def tail_of(rate, seg_column, seg_row):
    left = (PIECE - 1 - lax.broadcasted_iota(jnp.int32, (PIECE, 1), 0)).astype(F32)
    return jnp.where(seg_column == seg_row[:, PIECE - 1 :], jnp.exp(-rate * left), 0.0)


def reach_of(rate, seg_column, before):
    passed = (lax.broadcasted_iota(jnp.int32, (PIECE, 1), 0) + 1).astype(F32)
    return jnp.where(seg_column == before, jnp.exp(-rate * passed), 0.0)


def with_marks(total, seg_row):
    column = lax.broadcasted_iota(jnp.int32, total.shape, 1)
    marked = jnp.where(column == VW, seg_row[:, :1], jnp.where(column == VW + 1, seg_row[:, PIECE - 1 :], 0.0))
    return jnp.where(column < VW, total, marked).astype(BF)


def mark(states, offset):
    column = lax.broadcasted_iota(jnp.int32, (states.shape[0], 128), 1)
    return jnp.sum(jnp.where(column == VW - (VPAD - 128) + offset, states[:, VPAD - 128 :], 0.0), 1, keepdims=True)


def local_kernel(rates, seg_column, seg_row, base_key, base_value, helped_key, helped_value, _, keys, values, local, total):
    keys[...] = (base_key[...] + helped_key[...].astype(F32)).astype(BF)
    values[:, :VW] = (base_value[...] + helped_value[...].astype(F32)).astype(BF)
    values[:, VW:] = jnp.zeros((PIECE, VPAD - VW), BF)
    total[...] = jnp.zeros_like(total)
    for head in range(HEADS):
        begin, end = window(head)
        own = slice(head * KH, (head + 1) * KH)
        value = head_part(values, head, PIECE).astype(BF)
        key_tail = (keys[:, own].astype(F32) * tail_of(rates[head], seg_column[...], seg_row[...])).astype(BF)
        total[:, begin:end] += product_left(key_tail, value)
    local[...] = with_marks(total[...], seg_row[...])


def inner_kernel(rates, seg_column, seg_row, base_query, helped_query, keys, values, queries, inner, masked):
    queries[...] = (base_query[...] + helped_query[...].astype(F32)).astype(BF)
    inner[...] = jnp.zeros_like(inner)
    for head in range(HEADS):
        begin, end = window(head)
        own = slice(head * KH, (head + 1) * KH)
        scores = product_right(queries[:, own], keys[:, own])
        kept = (scores * decay_of(rates[head], seg_column[...], seg_row[...])).astype(BF)
        masked[head] = kept
        inner[:, begin:end] += product(kept, head_part(values, head, PIECE).astype(BF))


def scan_kernel(reverse, rates, states, *refs):
    out = refs[-1]
    column = lax.broadcasted_iota(jnp.int32, (8, VPAD), 1)
    rate = jnp.full((8, VPAD), rates[HEADS - 1], F32)
    for head in range(HEADS - 1):
        rate = jnp.where((column >= head * VH) & (column < (head + 1) * VH), rates[head], rate)
    factor = jnp.exp(-rate * PIECE)
    edges = [states[p, :, VPAD - 128 :].astype(F32) for p in range(NC)]

    def mark_of(p, offset):
        lane = lax.broadcasted_iota(jnp.int32, (8, 128), 1)
        return jnp.sum(jnp.where(lane == VW - (VPAD - 128) + offset, edges[p], 0.0), 1, keepdims=True)

    firsts = [mark_of(p, 0) for p in range(NC)]
    lasts = [mark_of(p, 1) for p in range(NC)]
    befores = [jnp.full((8, 1), -1.0, F32)] + lasts[:-1]
    carry = jnp.zeros((8, VPAD), F32)
    for k in range(NC):
        p = NC - 1 - k if reverse else k
        out[p] = jnp.where(column < VW, carry, befores[p]).astype(BF)
        keep = jnp.where((firsts[p] == lasts[p]) & (firsts[p] == befores[p]), factor, 0.0)
        carry = states[p].astype(F32) + keep * carry


def mix_kernel(
    rates, seg_column, queries, inner, incoming, base_gate, helped_gate, out_weight, others, _,
    gate, grouped, inverse, mixed, part, total, held, near, semaphores,
):
    copies = fetch([out_weight, part_of(others, 2)], [near, held], semaphores)
    gate[...] = base_gate[...] + helped_gate[...].astype(F32)
    before = mark(incoming[:16].astype(F32), 0)[:1]
    total[...] = inner[...]
    for head in range(HEADS):
        begin, end = window(head)
        own = slice(head * KH, (head + 1) * KH)
        across = product(queries[:, own], incoming[:, begin:end])
        total[:, begin:end] += jnp.where(
            inside(head, PIECE), reach_of(rates[head], seg_column[...], before) * across, 0.0
        )
    lane = lax.broadcasted_iota(jnp.int32, (PIECE, 128), 1)
    scales = jnp.zeros((PIECE, 128), F32)
    grouped[...] = jnp.zeros_like(grouped)
    for head in range(HEADS):
        begin, end = window(head)
        here = inside(head, PIECE)
        retained = jnp.where(here, total[:, begin:end], 0.0)
        center = jnp.where(here, retained - jnp.sum(retained, 1, keepdims=True) / VH, 0.0)
        scale = lax.rsqrt(jnp.sum(center * center, 1, keepdims=True) / VH + EPS)
        grouped[:, begin:end] += center * scale
        scales = jnp.where(lane == head, scale, scales)
    inverse[...] = scales
    mixed[:, :VW] = (jax.nn.silu(gate[...]) * grouped[:, :VW]).astype(BF)
    mixed[:, VW:] = jnp.zeros((PIECE, VPAD - VW), BF)
    copies[0].wait()
    part[:, :HALF] = product(mixed[:, :VW], near[...]).astype(BF)
    copies[1].wait()
    part[:, HALF:] = product_right(mixed[...], held[...]).astype(BF)


def mlp_kernel(
    shard, tokens, mine, theirs, gain, bias, base_hidden, helped_hidden, gate_weight, up_weight, others, _up, _low,
    middle, normed, inverse, low_own, grads, part,
    near_gate, near_up, far_gate, far_up, semaphores,
):
    copies = fetch(
        [gate_weight, part_of(others, 0), up_weight, part_of(others, 1)],
        [near_gate, far_gate, near_up, far_up],
        semaphores,
    )
    own, oth = own_first(shard[0], tokens[...].astype(F32))
    own = own + (mine[:, :HALF].astype(F32) + theirs[:, :HALF].astype(F32))
    oth = oth + (mine[:, HALF:].astype(F32) + theirs[:, HALF:].astype(F32))
    middle[:, :HALF] = own
    middle[:, HALF:] = oth
    own, oth, scale = normed_of(own, oth)
    gains, biases = own_first(shard[0], gain[...]), own_first(shard[0], bias[...])
    normed[:, :HALF] = own
    normed[:, HALF:] = oth
    inverse[...] = jnp.broadcast_to(scale, inverse.shape)
    low_own[...] = (own * gains[0] + biases[0]).astype(BF)
    low_oth = (oth * gains[1] + biases[1]).astype(BF)
    grads[:, 3 * VPAD :] = low_oth
    copies[0].wait()
    up_gate = product_right(low_own[...], near_gate[...])
    copies[1].wait()
    up_gate += product(low_oth, far_gate[:, :VW])
    copies[2].wait()
    up_vals = product_right(low_own[...], near_up[...])
    copies[3].wait()
    up_vals += product(low_oth, far_up[:, :VW])
    grad_hidden = base_hidden[...] + helped_hidden[...].astype(F32)
    sigma = jax.nn.sigmoid(up_gate)
    silu = up_gate * sigma
    none = jnp.zeros((PIECE, VPAD - VW), BF)
    for k, array in enumerate(
        (silu * up_vals, grad_hidden * up_vals * (sigma * (1.0 + up_gate * (1.0 - sigma))), grad_hidden * silu)
    ):
        grads[:, k * VPAD : k * VPAD + VW] = array.astype(BF)
        grads[:, k * VPAD + VW : (k + 1) * VPAD] = none
    total = product(grads[:, VPAD : VPAD + VW], near_gate[...])
    total += product(grads[:, 2 * VPAD : 2 * VPAD + VW], near_up[...])
    part[:, :HALF] = total.astype(BF)
    total = product_right(grads[:, VPAD : 2 * VPAD], far_gate[...])
    total += product_right(grads[:, 2 * VPAD : 3 * VPAD], far_up[...])
    part[:, HALF:] = total.astype(BF)


def down_kernel(own, theirs, weight, part):
    both = jnp.concatenate([own[:, :VW], theirs[:, :VW]], 0)
    part[...] = product(both, weight[...]).astype(BF)


def down_sum_kernel(mine, theirs, own, gone):
    own[...] = mine[:PIECE].astype(F32) + theirs[:PIECE].astype(F32)
    gone[...] = (mine[PIECE:].astype(F32) + theirs[PIECE:].astype(F32)).astype(BF)


def result_kernel(shard, middle, own, oth, out):
    total = [middle[:, :HALF] + own[...], middle[:, HALF:] + oth[...].astype(F32)]
    out[:, :HALF] = jnp.where(shard[0] == 0, total[0], total[1]).astype(BF)
    out[:, HALF:] = jnp.where(shard[0] == 0, total[1], total[0]).astype(BF)


def unmix_kernel(
    shard, rates, mine, theirs, normed, inverse, gain, up_own, up_oth, seg_column, seg_row, queries, incoming, gate,
    grouped, scales, out_weight, others,
    grad_middle, branch_own, branch_oth, vectors, grad_gate, grad_retained, term,
    held, total, near, far, semaphores,
):
    copies = fetch([out_weight, part_of(others, 2)], [near, far], semaphores)
    grads = [mine[:, cut].astype(F32) + theirs[:, cut].astype(F32) for cut in (slice(0, HALF), slice(HALF, WIDE))]
    norms = [normed[:, :HALF], normed[:, HALF:]]
    vectors[...] = jnp.zeros_like(vectors)
    for k in range(2):
        cut = slice(k * HALF, (k + 1) * HALF)
        vectors[0:1, cut] = jnp.sum(grads[k] * norms[k], 0, keepdims=True)
        vectors[1:2, cut] = jnp.sum(grads[k], 0, keepdims=True)
    back = norm_back(grads, own_first(shard[0], gain[...]), norms, inverse[:, :1])
    own, oth = up_own[...].astype(F32) + back[0], up_oth[...].astype(F32) + back[1]
    grad_middle[:, :HALF] = own
    grad_middle[:, HALF:] = oth
    branch_own[...] = own.astype(BF)
    branch_oth[...] = oth.astype(BF)
    before = mark(incoming[:16].astype(F32), 0)[:1]
    sigma = jax.nn.sigmoid(gate[...])
    copies[0].wait()
    grad_mixed = product_right(branch_own[...], near[...])
    copies[1].wait()
    grad_mixed += product(branch_oth[...], far[:, :VW])
    slope = sigma * (1.0 + gate[...] * (1.0 - sigma))
    none = jnp.zeros((PIECE, VPAD - VW), F32)
    grad_gate[:, :VW] = (grad_mixed * grouped[:, :VW] * slope).astype(BF)
    grad_gate[:, VW:] = none.astype(BF)
    held[:, :VW] = grad_mixed * (gate[...] * sigma)
    held[:, VW:] = none
    lane = lax.broadcasted_iota(jnp.int32, (PIECE, 128), 1)
    total[...] = jnp.zeros_like(total)
    for head in range(HEADS):
        begin, end = window(head)
        here = inside(head, PIECE)
        grad = head_part(held, head, PIECE)
        group = head_part(grouped, head, PIECE)
        scale = jnp.sum(jnp.where(lane == head, scales[...], 0.0), 1, keepdims=True)
        back = grad - jnp.sum(grad, 1, keepdims=True) / VH - group * (jnp.sum(grad * group, 1, keepdims=True) / VH)
        total[:PIECE, begin:end] += jnp.where(here, scale * back, 0.0)
    grad_retained[...] = total[:PIECE].astype(BF)
    total[...] = jnp.zeros_like(total)
    for head in range(HEADS):
        begin, end = window(head)
        own = slice(head * KH, (head + 1) * KH)
        reached = reach_of(rates[head], seg_column[...], before) * head_part(grad_retained, head, PIECE)
        total[:, begin:end] += product_left(queries[:, own], reached.astype(BF))
    term[...] = with_marks(total[...], seg_row[...])


def back_kernel(
    rates, seg_column, seg_row, queries, keys, values, masked, incoming, grad_retained, grad_gate, gb, mixed,
    gate_query, parcel, base_key, base_value,
):
    before = mark(incoming[:16].astype(F32), 0)[:1]
    gate_query[:, :VPAD] = grad_gate[...]
    base_value[...] = jnp.zeros_like(base_value)
    for head in range(HEADS):
        rate = rates[head]
        begin, end = window(head)
        own = slice(head * KH, (head + 1) * KH)
        value = head_part(values, head, PIECE).astype(BF)
        grad = head_part(grad_retained, head, PIECE).astype(BF)
        decay = decay_of(rate, seg_column[...], seg_row[...])
        reach = reach_of(rate, seg_column[...], before)
        grad_scores = (product_right(grad, value) * decay).astype(BF)
        grad_query = product(grad_scores, keys[:, own])
        grad_query += reach * product_right(grad, incoming[:, begin:end])
        gate_query[:, VPAD + head * KH : VPAD + (head + 1) * KH] = grad_query.astype(BF)
        base_key[:, own] = product_left(grad_scores, queries[:, own])
        base_value[:, begin:end] += product_left(masked[head], grad)
    parcel[:, :VPAD] = mixed[...]
    parcel[:, VPAD:] = gb[...]


def later_kernel(rates, seg_column, seg_row, keys, values, outgoing, base_key, base_value, _theirs, _early, out, total):
    total[...] = base_value[...]
    for head in range(HEADS):
        begin, end = window(head)
        own = slice(head * KH, (head + 1) * KH)
        value = head_part(values, head, PIECE).astype(BF)
        tail = tail_of(rates[head], seg_column[...], seg_row[...])
        grad_key = base_key[:, own] + tail * product_right(value, outgoing[:, begin:end])
        out[:, own] = grad_key.astype(BF)
        total[:, begin:end] += jnp.where(inside(head, PIECE), tail * product(keys[:, own], outgoing[:, begin:end]), 0.0)
    out[:, HALF:] = total[...].astype(BF)


def first_back_kernel(
    gate_query, gate_query_theirs, key_value, key_value_theirs, query_weight, key_weight, value_weight, gate_weight,
    part, helped,
):
    both = jnp.concatenate([gate_query[...], gate_query_theirs[...]], 0)
    total = product_right(both[:, VPAD : VPAD + HALF], query_weight[...])
    total += product(both[:, :VW], gate_weight[...])
    both = jnp.concatenate([key_value[...], key_value_theirs[...]], 0)
    total += product_right(both[:, :HALF], key_weight[...])
    total += product(both[:, HALF : HALF + VW], value_weight[...])
    part[...] = total[:PIECE].astype(BF)
    helped[...] = total[PIECE:].astype(BF)


def last_kernel(
    shard, mine, theirs, helped, helped_other, normed, inverse, gain, grad_middle, vectors, out, vec_own, vec_oth
):
    grads = [
        mine[...].astype(F32) + theirs[...].astype(F32),
        helped[...].astype(F32) + helped_other[...].astype(F32),
    ]
    norms = [normed[:, :HALF], normed[:, HALF:]]
    for k, vec in enumerate((vec_own, vec_oth)):
        cut = slice(k * HALF, (k + 1) * HALF)
        rows = [jnp.sum(grads[k] * norms[k], 0, keepdims=True), jnp.sum(grads[k], 0, keepdims=True)]
        rows += [vectors[0:1, cut], vectors[1:2, cut], jnp.zeros((12, HALF), F32)]
        vec[...] = jnp.concatenate(rows, 0).astype(BF)
    back = norm_back(grads, own_first(shard[0], gain[...]), norms, inverse[:, :1])
    total = [grad_middle[:, :HALF] + back[0], grad_middle[:, HALF:] + back[1]]
    out[:, :HALF] = jnp.where(shard[0] == 0, total[0], total[1])
    out[:, HALF:] = jnp.where(shard[0] == 0, total[1], total[0])


def rows_of(core):
    column = lax.broadcasted_iota(jnp.int32, (HALF // 2, HALF), 1)
    row = lax.broadcasted_iota(jnp.int32, (HALF // 2, HALF), 0)
    source = (row // BLOCK * 2 + core) * BLOCK + row % BLOCK
    return (column == source).astype(F32).astype(BF)


def rows_kernel(core, *refs):
    count = (len(refs) - 2) // 2
    for chosen, out in ((core[0], refs[-2]), (1 - core[0], refs[-1])):
        pick = rows_of(chosen)
        for k in range(2 * count):
            out[:, k * PIECE : (k + 1) * PIECE] = product_right(pick, refs[k][...]).astype(BF)


def rows_cut_kernel(start, core, own, sent, *refs):
    kept, gone = refs[-2:]
    for chosen, out in ((core[0], kept), (1 - core[0], gone)):
        pick = rows_of(chosen)
        out[:, :PIECE] = product_right(pick, own[...]).astype(BF)
        out[:, PIECE:] = product_right(pick, sent[:, start : start + HALF]).astype(BF)


def features_of(core, own, received):
    both = shape(HALF // 2, 2 * PIECE)
    kept, gone = run(rows_kernel, (both, both), [core], [own, received])
    return kept, core_swap(gone)


def features_in(core, own, sent, start, *later):
    both = shape(HALF // 2, 2 * PIECE)
    kept, gone = run(functools.partial(rows_cut_kernel, start), (both, both), [core], [own, sent], later)
    return kept, core_swap(gone)


def all_tokens(array, other):
    return (array, other, core_swap(array), core_swap(other))


def outer(features, groups, plan, chunk, width, vectors=None, core=None, later=(), flops=0):
    steps = len(plan)
    flat = [a for pair in features for a in pair]
    flat += [a for group in groups for a in group] + list(vectors or ())
    specs = [pl.BlockSpec((HALF // 2, 2 * PIECE), lambda i, c: (0, 0))] * (2 * len(features))
    for g in range(len(groups)):
        mine = [k for k in range(steps) if plan[k][1] == g]
        first, count, block = mine[0], len(mine), plan[mine[0]][2]
        assert mine == list(range(first, first + count))

        def place(i, c, first=first, count=count, block=block):
            return (0, block + jnp.clip(i - first, 0, count - 1))

        specs += [pl.BlockSpec((PIECE, chunk), place)] * 4
    specs += [pl.BlockSpec((16, HALF), lambda i, c: (0, 0))] * len(vectors or ())
    specs += [ANY] * len(later)
    flat += list(later)

    def chosen(step, column, choices):
        value = choices[plan[0][column]]
        for k in range(1, steps):
            if plan[k][column] != plan[k - 1][column]:
                value = jnp.where(step >= k, choices[plan[k][column]], value)
        return value

    def kernel(core, *refs):
        out = refs[-1]
        step = pl.program_id(0)
        count = 2 * len(features)
        left = [
            jnp.concatenate([refs[2 * k][...], refs[2 * k + 1][...]], 1) for k in range(len(features))
        ]
        right = [
            jnp.concatenate([refs[count + 4 * k + j][...] for j in range(4)], 0) for k in range(len(groups))
        ]
        out[...] = product(chosen(step, 0, left), chosen(step, 1, right)).astype(BF)
        if vectors is not None:

            @pl.when(step == steps - 1)
            def _():
                rows = refs[count + 4 * len(groups) :]
                total = (rows[0][...].astype(F32) + rows[1][...].astype(F32)) + (
                    rows[2][...].astype(F32) + rows[3][...].astype(F32)
                )
                column = lax.broadcasted_iota(jnp.int32, (16, 128), 1)
                row = lax.broadcasted_iota(jnp.int32, (16, 128), 0)
                shift = (column == row + 64).astype(F32).astype(BF)
                moved = product(product_right(rows_of(core[0]), total.astype(BF)).astype(BF), shift)
                out[:, chunk - 128 :] = (out[:, chunk - 128 :].astype(F32) + moved).astype(BF)

    if core is None:
        core = jnp.zeros((1,), jnp.int32)
    part = pl.pallas_call(
        kernel,
        out_shape=shape(HALF // 2, width),
        grid_spec=pltpu.PrefetchScalarGridSpec(
            num_scalar_prefetch=1,
            grid=(steps,),
            in_specs=specs,
            out_specs=pl.BlockSpec((HALF // 2, chunk), lambda i, c: (0, i)),
        ),
        compiler_params=pltpu.CompilerParams(vmem_limit_bytes=56 * 1024 * 1024),
        cost_estimate=pl.CostEstimate(flops=flops, bytes_accessed=0, transcendentals=0),
    )(core, *flat)
    return part.reshape(16, BLOCK, width)


def sum_kernel(parts, key, value, norms):
    total = parts[0].astype(F32)
    for k in range(1, 16):
        total += parts[k].astype(F32)
    key[...] = total[:, :HALF]
    value[...] = total[:, HALF : HALF + VW]
    norms[...] = total[:, HALF + VPAD - 128 :]


def sent(part):
    return lax.all_to_all(part, "ctx", 0, 0, axis_index_groups=PLANE, tiled=True)


def added(parts):
    return jnp.sum(parts.astype(F32), 0)


def body(
    tokens,
    segments,
    decay_rate,
    first_gain,
    first_bias,
    query_weight,
    key_weight,
    value_weight,
    gate_weight,
    out_weight,
    second_gain,
    second_bias,
    mlp_gate,
    mlp_up,
    mlp_down,
    upstream,
):
    shard = lax.axis_index("shard").astype(jnp.int32).reshape(1)
    ctx = lax.axis_index("ctx").astype(jnp.int32).reshape(1)
    core = ctx % 2
    tokens, upstream = tokens[0], upstream[0]
    value_turned, gate_turned, mlp_gate_turned, mlp_up_turned = value_weight.T, gate_weight.T, mlp_gate.T, mlp_up.T
    gain1, bias1, gain2, bias2 = first_gain[None], first_bias[None], second_gain[None], second_bias[None]
    seg = segments[0].astype(F32)
    seg_column, seg_row = seg[:, None], seg[None, :]
    weight = pltpu.VMEM((VW, HALF), BF)
    held = pltpu.VMEM((HALF, VPAD), BF)
    small = shape(PIECE, HALF)
    wide = shape(PIECE, WIDE)
    scale = shape(PIECE, 128, kind=F32)

    def dma(count):
        return pltpu.SemaphoreType.DMA((count,))

    normed1, inverse1, low1_own, low1_oth, packed = run(
        first_kernel,
        (shape(PIECE, WIDE, kind=F32), scale, small, small, shape(BLOCK, PACKED)),
        [ctx, shard],
        [tokens, gain1, bias1],
        [mlp_gate_turned, mlp_up_turned, out_weight],
        [pltpu.VMEM((GATHERED, VW, 128), BF), dma(GATHERED)],
    )
    low1_theirs = from_shard(low1_oth)
    packed = from_shard(after(packed, low1_theirs))
    theirs_key, theirs_value = run(
        help_kernel,
        (shape(PIECE, HALF, kind=F32), shape(PIECE, VW, kind=F32)),
        [],
        [low1_theirs, key_weight, value_turned],
    )
    helped_key, helped_value = from_shard(theirs_key), half_from_shard(theirs_value)
    theirs_query, theirs_gate = run(
        help_more_kernel,
        (shape(PIECE, HALF, kind=F32), shape(PIECE, VW, kind=F32)),
        [],
        [low1_theirs, query_weight, gate_turned],
    )
    helped_query, helped_gate = from_shard(theirs_query), half_from_shard(theirs_gate)
    base_query, base_key, base_value, base_gate = run(
        base_kernel,
        tuple(shape(PIECE, n, kind=F32) for n in (HALF, HALF, VW, VW)),
        [],
        [low1_own, query_weight, key_weight, value_turned, gate_turned],
        [theirs_key],
    )

    up_own, up_oth = run(turn_kernel, (small, small), [shard], [upstream])
    up_theirs = from_shard(up_oth)
    others = lax.all_gather(after(packed, theirs_value), "ctx", axis=0, tiled=True)


    def exchange(states, reverse, *before):
        mine = lax.all_to_all(states.reshape(NC, KH // NC, VPAD), "ctx", 0, 0, tiled=True)
        done = run(functools.partial(scan_kernel, reverse), shape(NC, KH // NC, VPAD), [decay_rate], [mine], before)
        return lax.all_to_all(done, "ctx", 0, 0, tiled=True).reshape(KH, VPAD), mine, done

    keys, values, local = run(
        local_kernel,
        (small, shape(PIECE, VPAD), shape(KH, VPAD)),
        [decay_rate],
        [seg_column, seg_row, base_key, base_value, helped_key, helped_value],
        [theirs_query],
        scratch=[pltpu.VMEM((KH, VPAD), F32)],
    )
    base_hidden, theirs_hidden = run(
        hidden_kernel,
        (shape(PIECE, VW, kind=F32), shape(PIECE, VW, kind=F32)),
        [],
        [up_own, up_theirs, mlp_down],
    )
    helped_hidden = half_from_shard(theirs_hidden)
    incoming, _, _ = exchange(local, False, helped_query, theirs_hidden)
    queries, inner, masked = run(
        inner_kernel,
        (small, shape(PIECE, VPAD, kind=F32), shape(HEADS, PIECE, PIECE)),
        [decay_rate],
        [seg_column, seg_row, base_query, helped_query, keys, values],
    )
    up_features = features_of(core, up_own, up_theirs)
    low1_features = features_of(core, low1_own, low1_theirs)
    gate_pre, grouped, scales, mixed, part = run(
        mix_kernel,
        (shape(PIECE, VW, kind=F32), shape(PIECE, VPAD, kind=F32), scale, shape(PIECE, VPAD), wide),
        [decay_rate],
        [seg_column, queries, inner, incoming, base_gate, helped_gate],
        [out_weight, others, helped_hidden],
        [pltpu.VMEM((PIECE, VPAD), F32), held, weight, dma(2)],
    )
    theirs = from_tp(part)
    middle, normed2, inverse2, low2_own, mlp_parts, part = run(
        mlp_kernel,
        (shape(PIECE, WIDE, kind=F32), shape(PIECE, WIDE, kind=F32), scale, small, shape(PIECE, 3 * VPAD + HALF), wide),
        [shard],
        [tokens, part, theirs, gain2, bias2, base_hidden, helped_hidden],
        [mlp_gate_turned, mlp_up_turned, others, up_features[1], low1_features[1]],
        [weight, weight, held, held, dma(4)],
    )
    theirs = from_tp(part)
    mlp_parts = after(mlp_parts, theirs)
    mlp_theirs = from_shard(mlp_parts)
    grad_middle, gb_own, gb_oth, vectors, grad_gate, grad_retained, term = run(
        unmix_kernel,
        (
            shape(PIECE, WIDE, kind=F32),
            small,
            small,
            shape(8, WIDE, kind=F32),
            shape(PIECE, VPAD),
            shape(PIECE, VPAD),
            shape(KH, VPAD),
        ),
        [shard, decay_rate],
        [part, theirs, normed2, inverse2, gain2, up_own, up_oth]
        + [seg_column, seg_row, queries, incoming, gate_pre, grouped, scales],
        [out_weight, others],
        [pltpu.VMEM((PIECE, VPAD), F32), pltpu.VMEM((KH, VPAD), F32), weight, held, dma(2)],
    )

    gate_query, parcel, base_key_grad, base_value_grad = run(
        back_kernel,
        (
            shape(PIECE, VPAD + HALF),
            shape(PIECE, VPAD + HALF),
            shape(PIECE, HALF, kind=F32),
            shape(PIECE, VPAD, kind=F32),
        ),
        [decay_rate],
        [seg_column, seg_row, queries, keys, values, masked, incoming, grad_retained, grad_gate, gb_oth, mixed],
    )
    parcel_theirs = from_shard(parcel)
    gate_query_theirs = from_shard(gate_query)
    outgoing, _, scanned = exchange(term, True, gate_query)
    mlp_parts, mlp_theirs = hold((mlp_parts, mlp_theirs), scanned)
    mlp_all = all_tokens(mlp_parts, mlp_theirs)
    early_part = outer(
        [
            up_features,
            features_in(core, low2_own, mlp_theirs, 3 * VPAD),
            features_in(core, gb_own, parcel_theirs, VPAD, scanned),
        ],
        [mlp_all, all_tokens(parcel, parcel_theirs)],
        [(0, 0, 0), (1, 0, 1), (1, 0, 2), (2, 1, 0)],
        VPAD,
        4 * VPAD,
    )
    early_part = after(early_part, outgoing)
    key_value = run(
        later_kernel,
        shape(PIECE, HALF + VPAD),
        [decay_rate],
        [seg_column, seg_row, keys, values, outgoing, base_key_grad, base_value_grad],
        [gate_query_theirs, early_part],
        scratch=[pltpu.VMEM((PIECE, VPAD), F32)],
    )
    key_value_theirs = from_shard(key_value)

    early = lax.psum_scatter(early_part, "ctx", scatter_dimension=0, axis_index_groups=PLANE, tiled=False)
    early = early.astype(F32)
    gate_query, gate_query_theirs = hold((gate_query, gate_query_theirs), key_value)
    gate_query_parts = sent(
        outer(
            [low1_features],
            [all_tokens(gate_query, gate_query_theirs)],
            [(0, 0, 0), (0, 0, 1)],
            (VPAD + HALF) // 2,
            VPAD + HALF,
            flops=100 * 10**9,
        )
    )
    first_weights = [query_weight, key_weight, value_turned, gate_turned]
    part, helped = run(
        first_back_kernel,
        (small, small),
        [],
        [gate_query, gate_query_theirs, key_value, key_value_theirs] + first_weights,
    )
    tokens_grad, vec_own, vec_oth = run(
        last_kernel,
        (shape(PIECE, WIDE, kind=F32), shape(16, HALF), shape(16, HALF)),
        [shard],
        [part, from_tp(part), from_shard(helped), lax.ppermute(helped, ("shard", "tp"), SHARD_TP)]
        + [normed1, inverse1, gain1, grad_middle, vectors],
    )
    sums = (
        vec_own,
        from_shard(vec_oth),
        core_swap(vec_own),
        lax.ppermute(vec_oth, ("shard", "ctx"), SHARD_CORE),
    )
    key_value_parts = sent(
        outer(
            [low1_features],
            [all_tokens(key_value, key_value_theirs)],
            [(0, 0, 0), (0, 0, 1)],
            (HALF + VPAD) // 2,
            HALF + VPAD,
            vectors=sums,
            core=core,
            later=(gate_query_parts,),
        )
    )

    part = run(down_kernel, shape(2 * PIECE, HALF), [], [mlp_parts, mlp_theirs, mlp_down])
    down_own, down_gone = run(
        down_sum_kernel, (shape(PIECE, HALF, kind=F32), small), [], [part, from_tp(part)]
    )
    layer_out = run(result_kernel, wide, [shard], [middle, down_own, from_shard(down_gone)])

    gate_query_sums = added(gate_query_parts)
    key_sums, value_sums, norms = run(
        sum_kernel,
        (shape(BLOCK, HALF, kind=F32), shape(BLOCK, VW, kind=F32), shape(BLOCK, 128, kind=F32)),
        [],
        [key_value_parts],
    )
    norms = norms[:, 64:68].T
    early = [early[:, k * VPAD : k * VPAD + VW] for k in range(4)]
    return (
        layer_out[None],
        tokens_grad[None],
        norms[0],
        norms[1],
        gate_query_sums[:, VPAD:],
        key_sums,
        value_sums,
        gate_query_sums[:, :VW],
        early[3].T,
        norms[2],
        norms[3],
        early[1],
        early[2],
        early[0].T,
    )


def solution(mesh):
    in_specs = (
        P("shard", "ctx", None),
        P("shard", "ctx"),
        P("tp"),
        P(),
        P(),
        P("shard", "tp"),
        P("shard", "tp"),
        P("shard", "tp"),
        P("shard", "tp"),
        P("tp", "shard"),
        P(),
        P(),
        P("shard", "tp"),
        P("shard", "tp"),
        P("tp", "shard"),
        P("shard", "ctx", None),
    )
    out_specs = (
        P("shard", "ctx", None),
        P("shard", "ctx", None),
        P(("shard", "ctx")),
        P(("shard", "ctx")),
        P(("shard", "ctx"), "tp"),
        P(("shard", "ctx"), "tp"),
        P(("shard", "ctx"), "tp"),
        P(("shard", "ctx"), "tp"),
        P("tp", ("shard", "ctx")),
        P(("shard", "ctx")),
        P(("shard", "ctx")),
        P(("shard", "ctx"), "tp"),
        P(("shard", "ctx"), "tp"),
        P("tp", ("shard", "ctx")),
    )
    return jax.shard_map(body, mesh=mesh, in_specs=in_specs, out_specs=out_specs, check_vma=False)
```
